256 devices in a mesh: grp: 8 (over z), tile: 32 (over x, y, core).
Axes of the slice: x: 4, y: 4, z: 8, core: 2. Of those that a mesh axis runs over, the one named last changes fastest.
Arguments:
- spot_terms: bfloat16 [65536, 1024], P('tile', 'grp'), may hold values from -6 to 6
- spot_weight: bfloat16 [65536], P('tile'), may hold values from 0.29882812 to 3
- spot_owner: int32 [65536, 1], P('tile'), may hold values from 0 to 31, as said below
- spot_cell: int32 [65536], P('tile'), may hold values from 0 to 1023
- col_coef: float32 [32, 1024], P('tile'), may hold values from 0.04 to 0.45
- row_coef: float32 [32, 1024], P('tile'), may hold values from 0.04 to 0.45
- tgt_coef: float32 [1024], P('grp'), may hold values from 0.03 to 0.24
- tgt_weight: float32 [1024], P('grp'), may hold values from 0.5 to 6
Outputs:
- new_plan: float32 [32, 1024, 1024], P('tile', None, 'grp')
The draws below stay inside these ranges and needn't reach their ends.
Inputs may be any that keep to these rules, and one draw needn't show every extreme that they name: `spot_owner`: among the 2048 spots of one device no owner is named more than 128 times, and in every device's block some owner is named exactly 128 times.
All inputs are finite; a program needn't handle non-finite values.
Results may differ from the reference program's by a relative error of at most 0.0003.
Values may be sent and summed in bfloat16 or wider, within the bound.
No kernel may reach another device: no remote copies, remote signals or barrier semaphores. Data moves between devices by JAX's collectives and lax.ppermute only.
A program may use at most 64 MiB of HBM per device.

```python
import math
import jax
import jax.numpy as jnp
from jax import lax

LAT_WIDTH = 1024
GROUP_COLS = 128
PATCH_ROW = 32
TILE_SOURCE_ROWS = 1
SPOT_DEV = 2048
HEAT_STEPS = 10
SCALING_ROUNDS = 5
CELLS_DEV = 1024
BAND_ROWS = 32
SPOTS = 65536
WINDOW = 1024
N_GRP = 8
N_TILE = 32


def spot_layout(key):
    base_count = SPOT_DEV // N_TILE
    half_owners = N_TILE // 2
    favour = jax.random.permutation(jax.random.fold_in(key, 101), N_TILE).astype(jnp.int32)
    pair_keys = jax.random.split(jax.random.fold_in(key, 102), N_TILE)
    orders = jax.vmap(lambda block_key: jax.random.permutation(block_key, N_TILE))(pair_keys).astype(jnp.int32)
    depth = jax.random.randint(jax.random.fold_in(key, 103), (N_TILE, half_owners), 0, base_count + 1, dtype=jnp.int32)
    depth = depth.at[:, 0].set(base_count)
    first_side = orders[:, 0::2]
    second_side = orders[:, 1::2]
    first_up = favour[first_side] > favour[second_side]
    upper_side = jnp.where(first_up, first_side, second_side)
    lower_side = jnp.where(first_up, second_side, first_side)
    block_rows = jnp.arange(N_TILE, dtype=jnp.int32)[:, None]
    counts = jnp.zeros((N_TILE, N_TILE), jnp.int32)
    counts = counts.at[block_rows, upper_side].set(base_count + depth)
    counts = counts.at[block_rows, lower_side].set(base_count - depth)
    ends = jnp.cumsum(counts, axis=1).astype(jnp.int32)
    position = jnp.arange(SPOT_DEV, dtype=jnp.int32)
    sorted_owner = jnp.sum((ends[:, None, :] <= position[None, :, None]).astype(jnp.int32), axis=2).astype(jnp.int32)
    shuffle_keys = jax.random.split(jax.random.fold_in(key, 104), N_TILE)
    shuffle = jax.vmap(lambda block_key: jax.random.permutation(block_key, SPOT_DEV))(shuffle_keys).astype(jnp.int32)
    owner = jnp.take_along_axis(sorted_owner, shuffle, axis=1).reshape(SPOTS).astype(jnp.int32)
    cell = jax.random.randint(jax.random.fold_in(key, 105), (SPOTS,), 0, CELLS_DEV, dtype=jnp.int32)
    return (owner, cell)


def draw_spot_owner(key, part):
    owner, cell = spot_layout(key)
    return owner[:, None].astype(jnp.int32)


def draw_spot_cell(key, part):
    owner, cell = spot_layout(key)
    return cell.astype(jnp.int32)


def draw_spot_terms(key, part):
    owner, cell = spot_layout(key)
    key = jax.random.fold_in(key, 5)
    band_row = (owner * TILE_SOURCE_ROWS + cell // LAT_WIDTH).astype(jnp.float32)
    lattice_col = (cell % LAT_WIDTH).astype(jnp.float32)
    offset_a = jax.random.uniform(jax.random.fold_in(key, 1), (), jnp.float32, 0.0, 2.0 * math.pi)
    offset_b = jax.random.uniform(jax.random.fold_in(key, 2), (), jnp.float32, 0.0, 2.0 * math.pi)
    alpha = math.pi * lattice_col / float(LAT_WIDTH) + 2.5 * math.pi * band_row / float(BAND_ROWS) + offset_a
    column = jnp.arange(WINDOW, dtype=jnp.int32)
    group_no = (column // GROUP_COLS).astype(jnp.float32)
    within = column % GROUP_COLS
    patch_p = (within // PATCH_ROW).astype(jnp.float32)
    patch_q = (within % PATCH_ROW).astype(jnp.float32)
    patch_rows = float(GROUP_COLS // PATCH_ROW)
    beta = math.pi * (1.5 * group_no / float(N_GRP) + 0.5 * patch_q / float(PATCH_ROW) + 0.25 * patch_p / patch_rows) + offset_b
    strength = 1.2 * float(CELLS_DEV) / float(SPOT_DEV)
    coherent = strength * jnp.cos(alpha[:, None] - beta[None, :])
    noise_key = jax.random.fold_in(key, 3)
    noise = jnp.clip(jax.random.normal(noise_key, (SPOTS, WINDOW), jnp.float32), -3.5, 3.5)
    return (noise + coherent).astype(jnp.bfloat16)


def draw_tgt_weight(key, part):
    key = jax.random.fold_in(key, 7)
    ramp = 1.0 + 2.0 * jnp.arange(WINDOW, dtype=jnp.float32) / float(max(WINDOW - 1, 1))
    base = jnp.exp(jax.random.uniform(key, (WINDOW,), jnp.float32, math.log(0.5), math.log(2.0)))
    return base * ramp


def levels(rng, dims, pieces, smallest, largest):
    level, own = 1.0, jax.random.fold_in(rng, 6)
    for axis_at, blocks in pieces:
        heights = jnp.exp(jax.random.uniform(jax.random.fold_in(own, axis_at), (blocks,), jnp.float32, smallest / len(pieces), largest / len(pieces)))
        level = level * jnp.repeat(heights, dims[axis_at] // blocks).reshape([-1 if axis == axis_at else 1 for axis in range(len(dims))])
    return level


def setup_inputs(seed: int = 0) -> dict:
    splits = jax.random.split(jax.random.key(seed), 9)
    spot_terms = draw_spot_terms(jax.random.fold_in(splits[8], 71), 0)
    spot_weight = jnp.clip(jnp.exp(math.log(3.0) - 2.306499 * jax.random.uniform(splits[1], (SPOTS,), jnp.float32) ** levels(splits[1], (SPOTS,), ((0, 32),), -0.2, 0.2)), 0.29882812, 3.0).astype(jnp.bfloat16)
    spot_owner = draw_spot_owner(jax.random.fold_in(splits[8], 71), 0)
    spot_cell = draw_spot_cell(jax.random.fold_in(splits[8], 71), 0)
    col_coef = jnp.clip(jnp.exp(math.log(0.45) - 2.4203681 * jax.random.uniform(splits[4], (BAND_ROWS, LAT_WIDTH), jnp.float32) ** levels(splits[4], (BAND_ROWS, LAT_WIDTH), ((0, 32),), -0.2, 0.2)), 0.04, 0.45)
    row_coef = jnp.clip(jnp.exp(math.log(0.45) - 2.4203681 * jax.random.uniform(splits[5], (BAND_ROWS, LAT_WIDTH), jnp.float32) ** levels(splits[5], (BAND_ROWS, LAT_WIDTH), ((0, 32),), -0.2, 0.2)), 0.04, 0.45)
    tgt_coef = jnp.clip(jnp.exp(math.log(0.24) - 2.0794415 * jax.random.uniform(splits[6], (WINDOW,), jnp.float32) ** levels(splits[6], (WINDOW,), ((0, 8),), -0.2, 0.2)), 0.03, 0.24)
    tgt_weight = draw_tgt_weight(jax.random.fold_in(splits[8], 71), 0)
    return {"spot_terms": spot_terms, "spot_weight": spot_weight, "spot_owner": spot_owner, "spot_cell": spot_cell, "col_coef": col_coef, "row_coef": row_coef, "tgt_coef": tgt_coef, "tgt_weight": tgt_weight}


EXPONENT_GAIN = 2.0


def shifted(values, offset, along_axis):
    length = values.shape[along_axis]
    filler_shape = list(values.shape)
    filler_shape[along_axis] = abs(offset)
    padding_value = jnp.zeros(filler_shape, values.dtype)
    if offset > 0:
        kept_part = lax.slice_in_dim(values, 0, length - offset, axis=along_axis)
        return jnp.concatenate([padding_value, kept_part], axis=along_axis)
    kept_part = lax.slice_in_dim(values, -offset, length, axis=along_axis)
    return jnp.concatenate([kept_part, padding_value], axis=along_axis)


def line_heat(values, coefficient, along_axis):
    def heat_once(step_index, current):
        beside = shifted(current, 1, along_axis) + shifted(current, -1, along_axis)
        return current + coefficient * (beside - 2.0 * current)
    return lax.fori_loop(0, HEAT_STEPS, heat_once, values)


def patch_heat(values, coefficient):
    last_axis = values.ndim - 1
    positions = jnp.arange(values.shape[-1], dtype=jnp.int32) % PATCH_ROW
    west_valid = positions > 0
    east_valid = positions < PATCH_ROW - 1

    def heat_once(step_index, current):
        western_edge = jnp.where(west_valid, shifted(current, 1, last_axis), 0.0)
        east_side = jnp.where(east_valid, shifted(current, -1, last_axis), 0.0)
        north_side = shifted(current, PATCH_ROW, last_axis)
        south_side = shifted(current, -PATCH_ROW, last_axis)
        beside = western_edge + east_side + north_side + south_side
        return current + coefficient * (beside - 4.0 * current)
    return lax.fori_loop(0, HEAT_STEPS, heat_once, values)


def reference(spot_terms, spot_weight, spot_owner, spot_cell, col_coef, row_coef, tgt_coef, tgt_weight):
    every_cell = BAND_ROWS * LAT_WIDTH
    cell_index = (spot_owner[:, 0] * CELLS_DEV + spot_cell).astype(jnp.int32)
    gathered = jax.ops.segment_sum(spot_terms.astype(jnp.float32), cell_index, num_segments=every_cell)
    cell_mass = jax.ops.segment_sum(spot_weight.astype(jnp.float32), cell_index, num_segments=every_cell)
    plan_field = gathered.reshape(BAND_ROWS, LAT_WIDTH, WINDOW)
    plan_field = line_heat(plan_field, col_coef[:, :, None], 1)
    plan_field = line_heat(plan_field, row_coef[:, :, None], 0)
    grouped = plan_field.reshape(BAND_ROWS, LAT_WIDTH, N_GRP, GROUP_COLS)
    grouped = patch_heat(grouped, tgt_coef.reshape(N_GRP, GROUP_COLS))
    gibbs_kernel = jnp.exp(EXPONENT_GAIN * grouped.reshape(every_cell, WINDOW))
    col_scale = jnp.ones((WINDOW,), jnp.float32)
    row_scale = jnp.zeros((every_cell,), jnp.float32)
    for scaling_round in range(SCALING_ROUNDS):
        row_sums = jnp.dot(gibbs_kernel, col_scale, precision=lax.Precision.HIGHEST)
        row_scale = cell_mass / row_sums
        col_sums = jnp.dot(row_scale, gibbs_kernel, precision=lax.Precision.HIGHEST)
        col_scale = tgt_weight / col_sums
    new_plan = row_scale[:, None] * gibbs_kernel * col_scale[None, :] * float(every_cell)
    return new_plan.reshape(BAND_ROWS, LAT_WIDTH, WINDOW)
```

```python
import functools

import jax
import jax.numpy as jnp
from jax import lax
from jax.experimental import pallas as pl
from jax.experimental.pallas import tpu as pltpu
from jax.sharding import PartitionSpec as P

PATCH_ROW = 32
HEAT_STEPS = 10
SCALING_ROUNDS = 5
EXPONENT_GAIN = 2.0
LANES = 128
CAP = 128
META = 16
F32 = jnp.float32
BF16 = jnp.bfloat16
NT = (((1,), (1,)), ((), ()))
EXACT = lax.Precision.HIGHEST


def iota(shape, axis):
    return lax.broadcasted_iota(jnp.int32, shape, axis)


def call(kernel, out_shape, operands, scratch=(), hbm=(), out_hbm=False):
    specs = []
    for i in range(len(operands)):
        space = pltpu.HBM if i in hbm else pltpu.VMEM
        specs.append(pl.BlockSpec(memory_space=space))
    out_space = pltpu.HBM if out_hbm else pltpu.VMEM
    outs = jax.tree.map(lambda _: pl.BlockSpec(memory_space=out_space), out_shape)
    return pl.pallas_call(
        kernel,
        out_shape=out_shape,
        in_specs=specs,
        out_specs=outs,
        scratch_shapes=list(scratch),
        compiler_params=pltpu.CompilerParams(vmem_limit_bytes=(60 if hbm else 40) * 2**20),
    )(*operands)


def onehot_rows(index, base, rows):
    n = index.shape[1]
    local = jnp.clip(index - float(base), -1.0, float(rows))
    local = jnp.broadcast_to(local, (16, n)).astype(BF16)
    row = iota((rows, LANES), 0).astype(F32).astype(BF16)
    row = row.reshape(rows // 16, 16, LANES)
    one = jnp.ones((rows // 16, 16, LANES), BF16)
    zero = jnp.zeros((rows // 16, 16, LANES), BF16)
    pieces = []
    for j in range(n // LANES):
        piece = local[None, :, j * LANES : (j + 1) * LANES]
        piece = jnp.broadcast_to(piece, row.shape)
        pieces.append(jnp.where(row == piece, one, zero).reshape(rows, LANES))
    return jnp.concatenate(pieces, axis=1)


def pack_kernel(
    owner_hbm, cell_hbm, weight_hbm, terms_hbm, out_hbm,
    out_ref, onehot_ref, owner_ref, cell_ref, weight_ref, terms_ref, sems, out_sems,
):
    tiles = out_ref.shape[0]
    spots = terms_ref.shape[0]
    block = 256
    pairs = [
        (owner_hbm, owner_ref), (cell_hbm, cell_ref), (weight_hbm, weight_ref), (terms_hbm, terms_ref),
    ]
    copies = [pltpu.make_async_copy(src, dst, sems.at[i]) for i, (src, dst) in enumerate(pairs)]
    for copy in copies:
        copy.start()
    before = (iota((block, block), 0) < iota((block, block), 1)).astype(F32).astype(BF16)
    copies[0].wait()
    owner = owner_ref[...]
    base = jnp.zeros((tiles, 1), F32)
    ranks = []
    for b in range(spots // block):
        own = owner[:, b * block : (b + 1) * block]
        member = (iota((tiles, block), 0) == own).astype(F32)
        inside = jnp.dot(member.astype(BF16), before, preferred_element_type=F32)
        ranks.append(jnp.sum(member * (inside + base), axis=0, keepdims=True))
        base = base + inside[:, block - 1 : block] + member[:, block - 1 : block]
    rank = jnp.concatenate(ranks, axis=1)
    slot = owner.astype(F32) * float(CAP) + rank
    for copy in copies[1:]:
        copy.wait()
    cell = cell_ref[...]
    high = (cell // 32).astype(F32)
    low = (cell % 32).astype(F32)
    weight = weight_ref[...].astype(F32)
    weight = jnp.concatenate([weight[i : i + 1] for i in range(spots // LANES)], axis=1)
    which = iota((tiles * 8, spots), 0)
    kind = which % 8
    value = jnp.where(kind == 0, weight, jnp.where(kind == 1, high, jnp.where(kind == 2, low, 0.0)))
    value = jnp.where(which // 8 == owner, value, 0.0).astype(BF16)
    onehot_ref[1, 0:CAP, :] = onehot_rows(rank, 0, CAP)
    meta = lax.dot_general(value, onehot_ref[1, 0:CAP, :], NT, preferred_element_type=F32)
    empty = jnp.zeros((8, LANES), F32)
    for t in range(tiles):
        out_ref[t, CAP : CAP + META, :] = jnp.concatenate(
            [meta[8 * t : 8 * t + 8], empty], axis=0
        ).astype(BF16)
    terms = terms_ref[...]
    leaving = []
    for chunk in range(tiles * CAP // 256):
        onehot_ref[chunk % 2] = onehot_rows(slot, chunk * 256, 256)
        rows = jnp.dot(onehot_ref[chunk % 2], terms, preferred_element_type=F32).astype(BF16)
        out_ref[2 * chunk, 0:CAP, :] = rows[:CAP]
        out_ref[2 * chunk + 1, 0:CAP, :] = rows[CAP:]
        both = pl.ds(2 * chunk, 2)
        leaving.append(
            pltpu.make_async_copy(out_ref.at[both], out_hbm.at[both], out_sems.at[chunk])
        )
        leaving[-1].start()
    for copy in leaving:
        copy.wait()


def column_of(row):
    return jnp.broadcast_to(row, (LANES, LANES)).T


def prep_kernel(col_ref, tgt_ref, ccol_ref, patch_ref):
    for t in range(col_ref.shape[1] // LANES):
        ccol_ref[t * LANES : (t + 1) * LANES, :] = column_of(
            col_ref[:, t * LANES : (t + 1) * LANES]
        )
    coef = column_of(tgt_ref[...])
    place = iota((LANES, LANES), 0)
    field = (place == iota((LANES, LANES), 1)).astype(F32)
    first = place % PATCH_ROW == 0
    last = place % PATCH_ROW == PATCH_ROW - 1
    zeros = jnp.zeros((PATCH_ROW, LANES), F32)
    for _ in range(HEAT_STEPS):
        west = jnp.where(first, 0.0, pltpu.roll(field, 1, 0))
        east = jnp.where(last, 0.0, pltpu.roll(field, LANES - 1, 0))
        north = jnp.concatenate([zeros, field[: LANES - PATCH_ROW]], axis=0)
        south = jnp.concatenate([field[PATCH_ROW:], zeros], axis=0)
        field = field + coef * (west + east + north + south - 4.0 * field)
    patch_ref[...] = field


def gather_kernel(msg_ref, ccol_ref, rcoef_ref, out_ref, onehot_ref, a_ref, b_ref):
    tiles = msg_ref.shape[0]
    cells = ccol_ref.shape[0]
    meta = msg_ref[:, CAP : CAP + META, :].astype(F32)
    weight = jnp.concatenate([meta[t, 0:1, :] for t in range(tiles)], axis=1)
    high = jnp.concatenate([meta[t, 1:2, :] for t in range(tiles)], axis=1)
    low = jnp.concatenate([meta[t, 2:3, :] for t in range(tiles)], axis=1)
    cell = high * 32.0 + low
    slots = tiles * CAP
    rows = msg_ref[:, 0:CAP, :].reshape(slots, LANES)
    pad = jnp.zeros((8, LANES), F32)
    for ref in (a_ref, b_ref):
        ref[0:8, :] = pad
        ref[8 + cells : 16 + cells, :] = pad
    for chunk in range(cells // 256):
        onehot_ref[chunk % 2] = onehot_rows(cell, chunk * 256, 256)
        a_ref[8 + 256 * chunk : 8 + 256 * (chunk + 1), :] = jnp.dot(
            onehot_ref[chunk % 2], rows, preferred_element_type=F32
        )
    blocks = cells // PATCH_ROW
    lane_shift = (lax.rem(lax.axis_index("tile"), 4) * 32).astype(F32)
    upper = jnp.where(iota((blocks, slots), 0).astype(F32) == high, weight, 0.0).astype(BF16)
    lower = (iota((LANES, slots), 0).astype(F32) == low + lane_shift).astype(F32).astype(BF16)
    mass = lax.dot_general(upper, lower, NT, preferred_element_type=F32)

    def heated(src, c, size):
        o = 8 + c * size
        mid = src[o : o + size, :]
        beside = src[o - 1 : o - 1 + size, :] + src[o + 1 : o + 1 + size, :]
        coef = ccol_ref[c * size : (c + 1) * size, :]
        return mid + coef * (beside - 2.0 * mid)

    def step(src, dst):
        size = 128
        for c in range(cells // size):
            dst[8 + c * size : 8 + (c + 1) * size, :] = heated(src, c, size)

    def two_steps(_, carry):
        step(a_ref, b_ref)
        step(b_ref, a_ref)
        return carry

    lax.fori_loop(0, HEAT_STEPS // 2 - 1, two_steps, 0)
    step(a_ref, b_ref)
    sub = iota((8, LANES), 0)
    for d in range(tiles):
        out_ref[d, 0:32, :] = heated(b_ref, d, 32)
        out_ref[d, 32:40, :] = jnp.where(
            sub == 0, rcoef_ref[d : d + 1, :], jnp.where(sub == 1, mass[d : d + 1, :], 0.0)
        )


def tile_of(parts):
    sub = iota((8, LANES), 0)
    out = jnp.broadcast_to(parts[0], (8, LANES))
    for t in range(1, 8):
        out = jnp.where(sub == t, parts[t], out)
    return out


def row_partials(kt_ref, vcol):
    parts = []
    for t in range(8):
        piece = kt_ref[:, t * LANES : (t + 1) * LANES].astype(F32)
        if vcol is not None:
            piece = piece * vcol
        parts.append(jnp.sum(piece, axis=0, keepdims=True))
    return tile_of(parts)


def band_kernel(
    msg_ref, patch_ref, weight_ref, kt_ref, short_ref, mass_ref, out_ref, coef_ref, field_ref
):
    tiles = msg_ref.shape[0]
    sub = iota((8, LANES), 0)
    mass = jnp.zeros((8, LANES), F32)
    coef = []
    for r in range(tiles):
        mass = mass + jnp.where(sub == r // 4, msg_ref[r, 33:34, :], 0.0)
    mass_ref[...] = mass
    for b in range(tiles // 8):
        coef.append(tile_of([msg_ref[8 * b + r, 32:33, :] for r in range(8)]))
    coef.append(jnp.zeros((LANES - tiles, LANES), F32))
    coef = jnp.concatenate(coef, axis=0).T
    for r in range(tiles):
        coef_ref[r, :, :] = jnp.broadcast_to(coef[0:32, r : r + 1], (32, LANES))
    zero = jnp.zeros((8, LANES), F32)
    for b in range(4):
        place = slice(8 * b, 8 * b + 8)

        def step(_, field):
            out = []
            for r in range(tiles):
                up = field[r - 1] if r > 0 else zero
                down = field[r + 1] if r < tiles - 1 else zero
                out.append(field[r] + coef_ref[r, place, :] * (up + down - 2.0 * field[r]))
            return tuple(out)

        field = lax.fori_loop(
            0, HEAT_STEPS, step, tuple(msg_ref[r, place, :] for r in range(tiles))
        )
        for r in range(tiles):
            field_ref[32 * r + 8 * b : 32 * r + 8 * b + 8, :] = field[r]
    smooth = lax.dot_general(
        patch_ref[...], field_ref[...], NT, preferred_element_type=F32, precision=EXACT
    )
    kernel = jnp.exp(EXPONENT_GAIN * smooth)
    kt_ref[...] = kernel
    short_ref[...] = kernel.astype(BF16)
    tile = row_partials(kt_ref, None)
    for g in range(out_ref.shape[0]):
        out_ref[g, 0:8, :] = tile
        out_ref[g, 8:16, :] = jnp.broadcast_to(weight_ref[...], (8, LANES))


def row_scale(msg_ref, mass_ref):
    total = msg_ref[0, 0:8, :]
    for g in range(1, msg_ref.shape[0]):
        total = total + msg_ref[g, 0:8, :]
    return mass_ref[...] / total


def scaled_columns(kt_ref, scale):
    pieces = [kt_ref[:, t * LANES : (t + 1) * LANES].astype(F32) for t in range(8)]
    return [piece * scale[t : t + 1, :] for t, piece in enumerate(pieces)]


def column_partials(kt_ref, scale):
    total = functools.reduce(lambda a, b: a + b, scaled_columns(kt_ref, scale))
    return jnp.sum(total.T, axis=0, keepdims=True)


def by_distance(msg_ref):
    groups = msg_ref.shape[0]
    me = lax.axis_index("grp")
    return tile_of([msg_ref[lax.rem(me + groups - k, groups), 8:9, :] for k in range(groups)])


def row_kernel(msg_ref, mass_ref, kt_ref, out_ref, weights_ref):
    weights_ref[...] = by_distance(msg_ref)
    column = column_partials(kt_ref, row_scale(msg_ref, mass_ref))
    for t in range(out_ref.shape[0]):
        out_ref[t, :, :] = column


def send_wide(out_ref, kernel_refs, scale):
    tile = tile_of([column_partials(ref, scale) for ref in kernel_refs])
    for t in range(out_ref.shape[0]):
        out_ref[t, :, :] = tile


def choose_kernel(even_ref, odd_ref, out_ref):
    odd = lax.rem(lax.axis_index("tile"), 2)

    @pl.when(odd == 0)
    def _():
        out_ref[...] = even_ref[...]

    @pl.when(odd == 1)
    def _():
        out_ref[...] = odd_ref[...]


def wide_row_sums(scale, kernel_refs):
    total = jnp.zeros((8, LANES), F32)
    for k, ref in enumerate(kernel_refs):
        total = total + row_partials(ref, column_of(scale[k : k + 1, :]))
    return total


def wide_row_kernel(msg_ref, mass_ref, *refs):
    kernel_refs, out_ref, later_ref = refs[:-2], refs[-2], refs[-1]
    scale = row_scale(msg_ref, mass_ref)
    send_wide(out_ref, kernel_refs, scale)
    later_ref[...] = scale * wide_row_sums(by_distance(msg_ref), kernel_refs)


def wide_row_scale(msg_ref, later_ref, weights_ref, kernel_refs):
    scale = column_scale([msg_ref[t] for t in range(msg_ref.shape[0])], weights_ref[...])
    return later_ref[...] / wide_row_sums(scale, kernel_refs)


def wide_round_kernel(msg_ref, later_ref, weights_ref, *refs):
    scale = wide_row_scale(msg_ref, later_ref, weights_ref, refs[:-1])
    send_wide(refs[-1], refs[:-1], scale)


def column_scale(parts, weight):
    while len(parts) > 1:
        parts = [a + b for a, b in zip(parts[0::2], parts[1::2])]
    return weight / parts[0]


def column_kernel(msg_ref, weight_ref, kt_ref, out_ref):
    scale = column_scale([msg_ref[t] for t in range(msg_ref.shape[0])], weight_ref[...])
    tile = row_partials(kt_ref, column_of(scale))
    for g in range(out_ref.shape[0]):
        out_ref[g, 0:8, :] = tile
        out_ref[g, 8:16, :] = jnp.broadcast_to(scale, (8, LANES))


def last_round_kernel(msg_ref, later_ref, weights_ref, *refs):
    out_ref = refs[-1]
    scale = wide_row_scale(msg_ref, later_ref, weights_ref, refs[:-1])
    pieces = scaled_columns(refs[0], scale)
    column = jnp.zeros((1, LANES), F32)
    for t in range(8):
        turned = pieces[t].T
        column = column + jnp.sum(turned, axis=0, keepdims=True)
        for r in range(4):
            out_ref[4 * t + r, 0:32, :] = turned[32 * r : 32 * r + 32]
    for r in range(out_ref.shape[0]):
        out_ref[r, 32:40, :] = jnp.broadcast_to(column, (8, LANES))


def plan_kernel(cell_count, msg_ref, weight_ref, out_hbm, plan_ref, sems):
    tiles = msg_ref.shape[0]
    scale = column_scale([msg_ref[t, 32:33, :] for t in range(tiles)], weight_ref[...])
    scale = scale * cell_count
    copies = []
    for d in range(tiles):
        plan_ref[0, 32 * d : 32 * d + 32, :] = msg_ref[d, 0:32, :] * scale
        if d % 8 == 7:
            rows = pl.ds(32 * (d - 7), 256)
            copies.append(
                pltpu.make_async_copy(
                    plan_ref.at[:, rows], out_hbm.at[:, rows], sems.at[d // 8]
                )
            )
            copies[-1].start()
    for copy in copies:
        copy.wait()


def swap(values, axis):
    return lax.all_to_all(values, axis, split_axis=0, concat_axis=0, tiled=True)


def body(spot_terms, spot_weight, spot_owner, spot_cell, col_coef, row_coef, tgt_coef, tgt_weight):
    tiles = lax.axis_size("tile")
    groups = lax.axis_size("grp")
    spots, columns = spot_terms.shape
    cells = col_coef.shape[1]
    shape = jax.ShapeDtypeStruct
    weight = tgt_weight.reshape(1, columns)

    packed = call(
        pack_kernel,
        shape((tiles, CAP + META, columns), BF16),
        [
            spot_owner.reshape(1, spots),
            spot_cell.reshape(1, spots),
            spot_weight.reshape(spots // LANES, LANES),
            spot_terms,
        ],
        scratch=[
            pltpu.VMEM((tiles, CAP + META, columns), BF16),
            pltpu.VMEM((2, 256, spots), BF16),
            pltpu.VMEM((1, spots), jnp.int32),
            pltpu.VMEM((1, spots), jnp.int32),
            pltpu.VMEM((spots // LANES, LANES), BF16),
            pltpu.VMEM((spots, columns), BF16),
            pltpu.SemaphoreType.DMA((4,)),
            pltpu.SemaphoreType.DMA((tiles * CAP // 256,)),
        ],
        hbm=(0, 1, 2, 3),
        out_hbm=True,
    )
    ccol, patch = call(
        prep_kernel,
        (shape((cells, LANES), F32), shape((LANES, LANES), F32)),
        [col_coef, tgt_coef.reshape(1, columns)],
    )
    rcoef = jnp.pad(row_coef.reshape(tiles, 32), ((0, 0), (0, LANES - 32)))
    got = swap(packed, "tile")
    sorted_field = call(
        gather_kernel,
        shape((tiles, 40, LANES), F32),
        [got, ccol, rcoef],
        scratch=[
            pltpu.VMEM((2, 256, tiles * CAP), BF16),
            pltpu.VMEM((cells + 16, LANES), F32),
            pltpu.VMEM((cells + 16, LANES), F32),
        ],
    )
    band = swap(sorted_field, "tile")
    tile = shape((8, LANES), F32)
    wide = shape((tiles, groups, LANES), F32)
    field = (columns, cells)
    kt, short, mass, rows = call(
        band_kernel,
        (shape(field, F32), shape(field, BF16), tile, shape((groups, 16, LANES), F32)),
        [band, patch, weight],
        scratch=[pltpu.VMEM((tiles, 32, LANES), F32), pltpu.VMEM((cells, LANES), F32)],
    )
    up = [(g, (g + 1) % groups) for g in range(groups)]
    down = [(g, (g - 1) % groups) for g in range(groups)]
    before = [kt, lax.ppermute(short, "grp", up)]
    after = [kt, lax.ppermute(short, "grp", down)]


    def forward(value):
        value, last, first = lax.optimization_barrier((value, before[-1], after[-1]))
        before[-1], after[-1] = last, first
        before.append(lax.ppermute(last, "grp", up))
        after.append(lax.ppermute(first, "grp", down))
        return value

    rows = forward(swap(rows, "grp"))
    leap = [
        (g * tiles + t, (g - 3 + 6 * (t % 2)) % groups * tiles + t)
        for g in range(groups)
        for t in range(tiles)
    ]
    opposite = call(choose_kernel, shape(field, BF16), [after[1], before[1]])
    opposite = lax.ppermute(opposite, ("grp", "tile"), leap)
    cols, weights = call(row_kernel, (shape((tiles, 1, LANES), F32), tile), [rows, mass, kt])
    cols = forward(swap(cols, "tile"))
    rows = call(column_kernel, shape((groups, 16, LANES), F32), [cols, weight, kt])
    rows, opposite = lax.optimization_barrier((rows, opposite))
    rows = swap(rows, "grp")
    every = before + [opposite] + after[:0:-1]
    cols, later = call(wide_row_kernel, (wide, tile), [rows, mass] + every)
    for _ in range(SCALING_ROUNDS - 3):
        cols = swap(cols, "tile")
        cols = call(wide_round_kernel, wide, [cols, later, weights] + every)
    cols = swap(cols, "tile")
    scaled = call(
        last_round_kernel, shape((tiles, 40, LANES), F32), [cols, later, weights] + every
    )
    scaled = swap(scaled, "tile")
    return call(
        functools.partial(plan_kernel, float(cells * tiles)),
        shape((1, cells, LANES), F32),
        [scaled, weight],
        scratch=[pltpu.VMEM((1, cells, LANES), F32), pltpu.SemaphoreType.DMA((tiles // 8,))],
        out_hbm=True,
    )


def solution(mesh):
    return jax.shard_map(
        body,
        mesh=mesh,
        in_specs=(
            P("tile", "grp"),
            P("tile"),
            P("tile", None),
            P("tile"),
            P("tile", None),
            P("tile", None),
            P("grp"),
            P("grp"),
        ),
        out_specs=P("tile", None, "grp"),
        check_vma=False,
    )
```

```python
import functools

import jax
import jax.numpy as jnp
from jax import lax
from jax.experimental import pallas as pl
from jax.experimental.pallas import tpu as pltpu
from jax.sharding import PartitionSpec as P

PATCH_ROW = 32
HEAT_STEPS = 10
SCALING_ROUNDS = 5
EXPONENT_GAIN = 2.0
LANES = 128
CAP = 128
META = 16
PART = 33
F32 = jnp.float32
BF16 = jnp.bfloat16
NT = (((1,), (1,)), ((), ()))
EXACT = lax.Precision.HIGHEST


def iota(shape, axis):
    return lax.broadcasted_iota(jnp.int32, shape, axis)


def call(kernel, out_shape, operands, scratch=(), hbm=(), out_hbm=False):
    specs = []
    for i in range(len(operands)):
        space = pltpu.HBM if i in hbm else pltpu.VMEM
        specs.append(pl.BlockSpec(memory_space=space))
    out_space = pltpu.HBM if out_hbm else pltpu.VMEM
    outs = jax.tree.map(lambda _: pl.BlockSpec(memory_space=out_space), out_shape)
    return pl.pallas_call(
        kernel,
        out_shape=out_shape,
        in_specs=specs,
        out_specs=outs,
        scratch_shapes=list(scratch),
        compiler_params=pltpu.CompilerParams(vmem_limit_bytes=(60 if hbm else 40) * 2**20),
    )(*operands)


def onehot_rows(index, base, rows):
    n = index.shape[1]
    local = jnp.clip(index - float(base), -1.0, float(rows))
    local = jnp.broadcast_to(local, (16, n)).astype(BF16)
    row = iota((rows, LANES), 0).astype(F32).astype(BF16)
    row = row.reshape(rows // 16, 16, LANES)
    one = jnp.ones((rows // 16, 16, LANES), BF16)
    zero = jnp.zeros((rows // 16, 16, LANES), BF16)
    pieces = []
    for j in range(n // LANES):
        piece = local[None, :, j * LANES : (j + 1) * LANES]
        piece = jnp.broadcast_to(piece, row.shape)
        pieces.append(jnp.where(row == piece, one, zero).reshape(rows, LANES))
    return jnp.concatenate(pieces, axis=1)


def pack_kernel(
    owner_hbm, cell_hbm, weight_hbm, terms_hbm, out_hbm,
    out_ref, onehot_ref, owner_ref, cell_ref, weight_ref, terms_ref, sems, out_sems,
):
    tiles = out_ref.shape[0]
    spots = terms_ref.shape[0]
    block = 256
    pairs = [
        (owner_hbm, owner_ref), (cell_hbm, cell_ref), (weight_hbm, weight_ref), (terms_hbm, terms_ref),
    ]
    copies = [pltpu.make_async_copy(src, dst, sems.at[i]) for i, (src, dst) in enumerate(pairs)]
    for copy in copies:
        copy.start()
    before = (iota((block, block), 0) < iota((block, block), 1)).astype(F32).astype(BF16)
    copies[0].wait()
    owner = owner_ref[...]
    base = jnp.zeros((tiles, 1), F32)
    ranks = []
    for b in range(spots // block):
        own = owner[:, b * block : (b + 1) * block]
        member = (iota((tiles, block), 0) == own).astype(F32)
        inside = jnp.dot(member.astype(BF16), before, preferred_element_type=F32)
        ranks.append(jnp.sum(member * (inside + base), axis=0, keepdims=True))
        base = base + inside[:, block - 1 : block] + member[:, block - 1 : block]
    rank = jnp.concatenate(ranks, axis=1)
    slot = owner.astype(F32) * float(CAP) + rank
    for copy in copies[1:]:
        copy.wait()
    cell = cell_ref[...]
    high = (cell // 32).astype(F32)
    low = (cell % 32).astype(F32)
    weight = weight_ref[...].astype(F32)
    weight = jnp.concatenate([weight[i : i + 1] for i in range(spots // LANES)], axis=1)
    which = iota((tiles * 8, spots), 0)
    kind = which % 8
    value = jnp.where(kind == 0, weight, jnp.where(kind == 1, high, jnp.where(kind == 2, low, 0.0)))
    value = jnp.where(which // 8 == owner, value, 0.0).astype(BF16)
    onehot_ref[0:CAP, :] = onehot_rows(rank, 0, CAP)
    meta = lax.dot_general(value, onehot_ref[0:CAP, :], NT, preferred_element_type=F32)
    empty = jnp.zeros((8, LANES), F32)
    for t in range(tiles):
        out_ref[t, CAP : CAP + META, :] = jnp.concatenate(
            [meta[8 * t : 8 * t + 8], empty], axis=0
        ).astype(BF16)
    terms = terms_ref[...]
    leaving = []
    for chunk in range(tiles * CAP // 256):
        onehot_ref[...] = onehot_rows(slot, chunk * 256, 256)
        rows = jnp.dot(onehot_ref[...], terms, preferred_element_type=F32).astype(BF16)
        out_ref[2 * chunk, 0:CAP, :] = rows[:CAP]
        out_ref[2 * chunk + 1, 0:CAP, :] = rows[CAP:]
        both = pl.ds(2 * chunk, 2)
        leaving.append(
            pltpu.make_async_copy(out_ref.at[both], out_hbm.at[both], out_sems.at[chunk])
        )
        leaving[-1].start()
    for copy in leaving:
        copy.wait()


def column_of(row):
    return jnp.broadcast_to(row, (LANES, LANES)).T


def prep_kernel(col_ref, tgt_ref, ccol_ref, patch_ref):
    for t in range(col_ref.shape[1] // LANES):
        ccol_ref[t * LANES : (t + 1) * LANES, :] = column_of(
            col_ref[:, t * LANES : (t + 1) * LANES]
        )
    coef = column_of(tgt_ref[...])
    place = iota((LANES, LANES), 0)
    field = (place == iota((LANES, LANES), 1)).astype(F32)
    first = place % PATCH_ROW == 0
    last = place % PATCH_ROW == PATCH_ROW - 1
    zeros = jnp.zeros((PATCH_ROW, LANES), F32)
    for _ in range(HEAT_STEPS):
        west = jnp.where(first, 0.0, pltpu.roll(field, 1, 0))
        east = jnp.where(last, 0.0, pltpu.roll(field, LANES - 1, 0))
        north = jnp.concatenate([zeros, field[: LANES - PATCH_ROW]], axis=0)
        south = jnp.concatenate([field[PATCH_ROW:], zeros], axis=0)
        field = field + coef * (west + east + north + south - 4.0 * field)
    patch_ref[...] = field


def gather_kernel(msg_ref, ccol_ref, rcoef_ref, out_ref, onehot_ref, a_ref, b_ref):
    tiles = msg_ref.shape[0]
    cells = ccol_ref.shape[0]
    meta = msg_ref[:, CAP : CAP + META, :].astype(F32)
    weight = jnp.concatenate([meta[t, 0:1, :] for t in range(tiles)], axis=1)
    high = jnp.concatenate([meta[t, 1:2, :] for t in range(tiles)], axis=1)
    low = jnp.concatenate([meta[t, 2:3, :] for t in range(tiles)], axis=1)
    cell = high * 32.0 + low
    slots = tiles * CAP
    rows = msg_ref[:, 0:CAP, :].reshape(slots, LANES)
    pad = jnp.zeros((8, LANES), F32)
    for ref in (a_ref, b_ref):
        ref[0:8, :] = pad
        ref[8 + cells : 16 + cells, :] = pad
    for chunk in range(cells // 256):
        onehot_ref[...] = onehot_rows(cell, chunk * 256, 256)
        a_ref[8 + 256 * chunk : 8 + 256 * (chunk + 1), :] = jnp.dot(
            onehot_ref[...], rows, preferred_element_type=F32
        )
    blocks = cells // PATCH_ROW
    lane_shift = (lax.rem(lax.axis_index("tile"), 4) * 32).astype(F32)
    upper = jnp.where(iota((blocks, slots), 0).astype(F32) == high, weight, 0.0).astype(BF16)
    lower = (iota((LANES, slots), 0).astype(F32) == low + lane_shift).astype(F32).astype(BF16)
    mass = lax.dot_general(upper, lower, NT, preferred_element_type=F32)

    def step(src, dst):
        size = 128
        for c in range(cells // size):
            o = 8 + c * size
            mid = src[o : o + size, :]
            beside = src[o - 1 : o - 1 + size, :] + src[o + 1 : o + 1 + size, :]
            coef = ccol_ref[c * size : (c + 1) * size, :]
            dst[o : o + size, :] = mid + coef * (beside - 2.0 * mid)

    def two_steps(_, carry):
        step(a_ref, b_ref)
        step(b_ref, a_ref)
        return carry

    lax.fori_loop(0, HEAT_STEPS // 2, two_steps, 0)
    shift = lax.rem(lax.axis_index("tile") + 2, 4) * 32
    extra = mass + pltpu.roll(rcoef_ref[...], shift, 1)
    for d in range(tiles):
        out_ref[PART * d : PART * d + 32, :] = a_ref[8 + 32 * d : 40 + 32 * d, :]
        out_ref[PART * d + 32 : PART * d + 33, :] = extra[d : d + 1, :]


def tile_of(parts):
    sub = iota((8, LANES), 0)
    out = jnp.broadcast_to(parts[0], (8, LANES))
    for t in range(1, 8):
        out = jnp.where(sub == t, parts[t], out)
    return out


def row_partials(kt_ref, vcol):
    parts = []
    for t in range(8):
        piece = kt_ref[:, t * LANES : (t + 1) * LANES].astype(F32)
        if vcol is not None:
            piece = piece * vcol
        parts.append(jnp.sum(piece, axis=0, keepdims=True))
    return tile_of(parts)


def band_kernel(
    msg_ref, patch_ref, weight_ref, kt_ref, short_ref, mass_ref, out_ref, coef_ref, field_ref
):
    tiles = msg_ref.shape[0] // PART
    owner = iota((8, LANES), 0) * 4 + iota((8, LANES), 1) // 32
    extra = [msg_ref[PART * r + 32 : PART * r + 33, :] for r in range(tiles)]
    mass = jnp.zeros((8, LANES), F32)
    coef = []
    for r in range(tiles):
        mass = jnp.where(owner == r, extra[r], mass)
    mass_ref[...] = mass
    for b in range(tiles // 8):
        coef.append(tile_of(extra[8 * b : 8 * b + 8]))
    coef.append(jnp.zeros((LANES - tiles, LANES), F32))
    coef = jnp.concatenate(coef, axis=0).T
    for r in range(tiles):
        at = 32 * ((r + 2) % 4)
        coef_ref[r, :, :] = jnp.broadcast_to(coef[at : at + 32, r : r + 1], (32, LANES))
    zero = jnp.zeros((8, LANES), F32)
    for b in range(4):
        place = slice(8 * b, 8 * b + 8)

        def step(_, field):
            out = []
            for r in range(tiles):
                up = field[r - 1] if r > 0 else zero
                down = field[r + 1] if r < tiles - 1 else zero
                out.append(field[r] + coef_ref[r, place, :] * (up + down - 2.0 * field[r]))
            return tuple(out)

        field = lax.fori_loop(
            0, HEAT_STEPS, step, tuple(msg_ref[PART * r + 8 * b : PART * r + 8 * b + 8, :] for r in range(tiles))
        )
        for r in range(tiles):
            field_ref[32 * r + 8 * b : 32 * r + 8 * b + 8, :] = field[r]
    smooth = lax.dot_general(
        patch_ref[...], field_ref[...], NT, preferred_element_type=F32, precision=EXACT
    )
    kernel = jnp.exp(EXPONENT_GAIN * smooth)
    kt_ref[...] = kernel
    short_ref[...] = kernel.astype(BF16)
    tile = row_partials(kt_ref, None)
    for g in range(out_ref.shape[0]):
        out_ref[g, 0:8, :] = tile
        out_ref[g, 8:16, :] = jnp.broadcast_to(weight_ref[...], (8, LANES))


def row_scale(msg_ref, mass_ref):
    total = msg_ref[0, 0:8, :]
    for g in range(1, msg_ref.shape[0]):
        total = total + msg_ref[g, 0:8, :]
    return mass_ref[...] / total


def scaled_columns(kt_ref, scale):
    pieces = [kt_ref[:, t * LANES : (t + 1) * LANES].astype(F32) for t in range(8)]
    return [piece * scale[t : t + 1, :] for t, piece in enumerate(pieces)]


def column_partials(kt_ref, scale):
    total = functools.reduce(lambda a, b: a + b, scaled_columns(kt_ref, scale))
    return jnp.sum(total.T, axis=0, keepdims=True)


def by_distance(msg_ref):
    groups = msg_ref.shape[0]
    me = lax.axis_index("grp")
    return tile_of([msg_ref[lax.rem(me + groups - k, groups), 8:9, :] for k in range(groups)])


def row_kernel(msg_ref, mass_ref, kt_ref, out_ref, weights_ref):
    weights_ref[...] = by_distance(msg_ref)
    column = column_partials(kt_ref, row_scale(msg_ref, mass_ref))
    for t in range(out_ref.shape[0]):
        out_ref[t, :, :] = column


def send_wide(out_ref, kernel_refs, scale):
    tile = tile_of([column_partials(ref, scale) for ref in kernel_refs])
    for t in range(out_ref.shape[0]):
        out_ref[t, :, :] = tile


def choose_kernel(even_ref, odd_ref, out_ref):
    odd = lax.rem(lax.axis_index("tile"), 2)

    @pl.when(odd == 0)
    def _():
        out_ref[...] = even_ref[...]

    @pl.when(odd == 1)
    def _():
        out_ref[...] = odd_ref[...]


def wide_row_sums(scale, kernel_refs):
    total = jnp.zeros((8, LANES), F32)
    for k, ref in enumerate(kernel_refs):
        total = total + row_partials(ref, column_of(scale[k : k + 1, :]))
    return total


def wide_row_kernel(msg_ref, mass_ref, *refs):
    kernel_refs, out_ref, later_ref = refs[:-2], refs[-2], refs[-1]
    scale = row_scale(msg_ref, mass_ref)
    send_wide(out_ref, kernel_refs, scale)
    later_ref[...] = scale * wide_row_sums(by_distance(msg_ref), kernel_refs)


def wide_row_scale(msg_ref, later_ref, weights_ref, kernel_refs):
    scale = column_scale([msg_ref[t] for t in range(msg_ref.shape[0])], weights_ref[...])
    return later_ref[...] / wide_row_sums(scale, kernel_refs)


def wide_round_kernel(msg_ref, later_ref, weights_ref, *refs):
    scale = wide_row_scale(msg_ref, later_ref, weights_ref, refs[:-1])
    send_wide(refs[-1], refs[:-1], scale)


def column_scale(parts, weight):
    while len(parts) > 1:
        parts = [a + b for a, b in zip(parts[0::2], parts[1::2])]
    return weight / parts[0]


def column_kernel(msg_ref, weight_ref, kt_ref, out_ref):
    scale = column_scale([msg_ref[t] for t in range(msg_ref.shape[0])], weight_ref[...])
    tile = row_partials(kt_ref, column_of(scale))
    for g in range(out_ref.shape[0]):
        out_ref[g, 0:8, :] = tile
        out_ref[g, 8:16, :] = jnp.broadcast_to(scale, (8, LANES))


def last_round_kernel(msg_ref, later_ref, weights_ref, *refs):
    out_ref = refs[-1]
    scale = wide_row_scale(msg_ref, later_ref, weights_ref, refs[:-1])
    pieces = scaled_columns(refs[0], scale)
    column = jnp.zeros((1, LANES), F32)
    for t in range(8):
        turned = pieces[t].T
        column = column + jnp.sum(turned, axis=0, keepdims=True)
        for r in range(4):
            at = PART * (4 * t + r)
            out_ref[at : at + 32, :] = turned[32 * r : 32 * r + 32]
    for at in range(32, out_ref.shape[0], PART):
        out_ref[at : at + 1, :] = column


def plan_kernel(cell_count, msg_ref, weight_ref, out_ref):
    tiles = msg_ref.shape[0] // PART
    sums = [msg_ref[PART * t + 32 : PART * t + 33, :] for t in range(tiles)]
    scale = column_scale(sums, weight_ref[...]) * cell_count
    for d in range(tiles):
        out_ref[0, 32 * d : 32 * d + 32, :] = msg_ref[PART * d : PART * d + 32, :] * scale


def swap(values, axis):
    return lax.all_to_all(values, axis, split_axis=0, concat_axis=0, tiled=True)


def swap_parts(parts, axis):
    size = lax.axis_size(axis)
    return swap(parts.reshape(size, PART, 1, LANES), axis).reshape(size * PART, LANES)


def body(spot_terms, spot_weight, spot_owner, spot_cell, col_coef, row_coef, tgt_coef, tgt_weight):
    tiles = lax.axis_size("tile")
    groups = lax.axis_size("grp")
    spots, columns = spot_terms.shape
    cells = col_coef.shape[1]
    shape = jax.ShapeDtypeStruct
    weight = tgt_weight.reshape(1, columns)

    packed = call(
        pack_kernel,
        shape((tiles, CAP + META, columns), BF16),
        [
            spot_owner.reshape(1, spots),
            spot_cell.reshape(1, spots),
            spot_weight.reshape(spots // LANES, LANES),
            spot_terms,
        ],
        scratch=[
            pltpu.VMEM((tiles, CAP + META, columns), BF16),
            pltpu.VMEM((256, spots), BF16),
            pltpu.VMEM((1, spots), jnp.int32),
            pltpu.VMEM((1, spots), jnp.int32),
            pltpu.VMEM((spots // LANES, LANES), BF16),
            pltpu.VMEM((spots, columns), BF16),
            pltpu.SemaphoreType.DMA((4,)),
            pltpu.SemaphoreType.DMA((tiles * CAP // 256,)),
        ],
        hbm=(0, 1, 2, 3),
        out_hbm=True,
    )
    ccol, patch = call(
        prep_kernel,
        (shape((cells, LANES), F32), shape((LANES, LANES), F32)),
        [col_coef, tgt_coef.reshape(1, columns)],
    )
    rcoef = jnp.pad(row_coef.reshape(tiles, 32), ((0, 0), (0, LANES - 32)))
    got = swap(packed, "tile")
    sorted_field = call(
        gather_kernel,
        shape((tiles * PART, LANES), F32),
        [got, ccol, rcoef],
        scratch=[
            pltpu.VMEM((256, tiles * CAP), BF16),
            pltpu.VMEM((cells + 16, LANES), F32),
            pltpu.VMEM((cells + 16, LANES), F32),
        ],
    )
    band = swap_parts(sorted_field, "tile")
    tile = shape((8, LANES), F32)
    wide = shape((tiles, groups, LANES), F32)
    field = (columns, cells)
    kt, short, mass, rows = call(
        band_kernel,
        (shape(field, F32), shape(field, BF16), tile, shape((groups, 16, LANES), F32)),
        [band, patch, weight],
        scratch=[pltpu.VMEM((tiles, 32, LANES), F32), pltpu.VMEM((cells, LANES), F32)],
    )
    up = [(g, (g + 1) % groups) for g in range(groups)]
    down = [(g, (g - 1) % groups) for g in range(groups)]
    before = [kt, lax.ppermute(short, "grp", up)]
    after = [kt, lax.ppermute(short, "grp", down)]


    def forward(value):
        value, last, first = lax.optimization_barrier((value, before[-1], after[-1]))
        before[-1], after[-1] = last, first
        before.append(lax.ppermute(last, "grp", up))
        after.append(lax.ppermute(first, "grp", down))
        return value

    rows = forward(swap(rows, "grp"))
    leap = [
        (g * tiles + t, (g - 3 + 6 * (t % 2)) % groups * tiles + t)
        for g in range(groups)
        for t in range(tiles)
    ]
    opposite = call(choose_kernel, shape(field, BF16), [after[1], before[1]])
    opposite = lax.ppermute(opposite, ("grp", "tile"), leap)
    cols, weights = call(row_kernel, (shape((tiles, 1, LANES), F32), tile), [rows, mass, kt])
    cols = forward(swap(cols, "tile"))
    rows = call(column_kernel, shape((groups, 16, LANES), F32), [cols, weight, kt])
    rows, opposite = lax.optimization_barrier((rows, opposite))
    rows = swap(rows, "grp")
    every = before + [opposite] + after[:0:-1]
    cols, later = call(wide_row_kernel, (wide, tile), [rows, mass] + every)
    for _ in range(SCALING_ROUNDS - 3):
        cols = swap(cols, "tile")
        cols = call(wide_round_kernel, wide, [cols, later, weights] + every)
    cols = swap(cols, "tile")
    scaled = call(
        last_round_kernel, shape((tiles * PART, LANES), F32), [cols, later, weights] + every
    )
    scaled = swap_parts(scaled, "tile")
    return call(
        functools.partial(plan_kernel, float(cells * tiles)),
        shape((1, cells, LANES), F32),
        [scaled, weight],
    )


def solution(mesh):
    return jax.shard_map(
        body,
        mesh=mesh,
        in_specs=(
            P("tile", "grp"),
            P("tile"),
            P("tile", None),
            P("tile"),
            P("tile", None),
            P("tile", None),
            P("grp"),
            P("grp"),
        ),
        out_specs=P("tile", None, "grp"),
        check_vma=False,
    )
```

```python
import functools

import jax
import jax.numpy as jnp
from jax import lax
from jax.experimental import pallas as pl
from jax.experimental.pallas import tpu as pltpu
from jax.sharding import PartitionSpec as P

PATCH_ROW = 32
HEAT_STEPS = 10
SCALING_ROUNDS = 5
EXPONENT_GAIN = 2.0
LANES = 128
CAP = 128
META = 16
PART = 33
F32 = jnp.float32
BF16 = jnp.bfloat16
NT = (((1,), (1,)), ((), ()))
EXACT = lax.Precision.HIGHEST


def iota(shape, axis):
    return lax.broadcasted_iota(jnp.int32, shape, axis)


def call(kernel, out_shape, operands, scratch=(), hbm=(), out_hbm=False):
    specs = []
    for i in range(len(operands)):
        space = pltpu.HBM if i in hbm else pltpu.VMEM
        specs.append(pl.BlockSpec(memory_space=space))
    out_space = pltpu.HBM if out_hbm else pltpu.VMEM
    outs = jax.tree.map(lambda _: pl.BlockSpec(memory_space=out_space), out_shape)
    return pl.pallas_call(
        kernel,
        out_shape=out_shape,
        in_specs=specs,
        out_specs=outs,
        scratch_shapes=list(scratch),
        compiler_params=pltpu.CompilerParams(vmem_limit_bytes=(60 if hbm else 40) * 2**20),
    )(*operands)


def onehot_rows(index, base, rows):
    n = index.shape[1]
    local = jnp.clip(index - float(base), -1.0, float(rows))
    local = jnp.broadcast_to(local, (16, n)).astype(BF16)
    row = iota((rows, LANES), 0).astype(F32).astype(BF16)
    row = row.reshape(rows // 16, 16, LANES)
    one = jnp.ones((rows // 16, 16, LANES), BF16)
    zero = jnp.zeros((rows // 16, 16, LANES), BF16)
    pieces = []
    for j in range(n // LANES):
        piece = local[None, :, j * LANES : (j + 1) * LANES]
        piece = jnp.broadcast_to(piece, row.shape)
        pieces.append(jnp.where(row == piece, one, zero).reshape(rows, LANES))
    return jnp.concatenate(pieces, axis=1)


def pack_kernel(
    owner_hbm, cell_hbm, weight_hbm, terms_hbm, out_hbm,
    out_ref, onehot_ref, owner_ref, cell_ref, weight_ref, terms_ref, sems, out_sems,
):
    tiles = out_ref.shape[0]
    spots = terms_ref.shape[0]
    block = 256
    pairs = [
        (owner_hbm, owner_ref), (cell_hbm, cell_ref), (weight_hbm, weight_ref), (terms_hbm, terms_ref),
    ]
    copies = [pltpu.make_async_copy(src, dst, sems.at[i]) for i, (src, dst) in enumerate(pairs)]
    for copy in copies:
        copy.start()
    before = (iota((block, block), 0) < iota((block, block), 1)).astype(F32).astype(BF16)
    copies[0].wait()
    owner = owner_ref[...]
    base = jnp.zeros((tiles, 1), F32)
    ranks = []
    for b in range(spots // block):
        own = owner[:, b * block : (b + 1) * block]
        member = (iota((tiles, block), 0) == own).astype(F32)
        inside = jnp.dot(member.astype(BF16), before, preferred_element_type=F32)
        ranks.append(jnp.sum(member * (inside + base), axis=0, keepdims=True))
        base = base + inside[:, block - 1 : block] + member[:, block - 1 : block]
    rank = jnp.concatenate(ranks, axis=1)
    slot = owner.astype(F32) * float(CAP) + rank
    for copy in copies[1:]:
        copy.wait()
    cell = cell_ref[...]
    high = (cell // 32).astype(F32)
    low = (cell % 32).astype(F32)
    weight = weight_ref[...].astype(F32)
    weight = jnp.concatenate([weight[i : i + 1] for i in range(spots // LANES)], axis=1)
    which = iota((tiles * 8, spots), 0)
    kind = which % 8
    value = jnp.where(kind == 0, weight, jnp.where(kind == 1, high, jnp.where(kind == 2, low, 0.0)))
    value = jnp.where(which // 8 == owner, value, 0.0).astype(BF16)
    onehot_ref[0:CAP, :] = onehot_rows(rank, 0, CAP)
    meta = lax.dot_general(value, onehot_ref[0:CAP, :], NT, preferred_element_type=F32)
    empty = jnp.zeros((8, LANES), F32)
    for t in range(tiles):
        out_ref[t, CAP : CAP + META, :] = jnp.concatenate(
            [meta[8 * t : 8 * t + 8], empty], axis=0
        ).astype(BF16)
    terms = terms_ref[...]
    leaving = []
    for chunk in range(tiles * CAP // 256):
        onehot_ref[...] = onehot_rows(slot, chunk * 256, 256)
        rows = jnp.dot(onehot_ref[...], terms, preferred_element_type=F32).astype(BF16)
        out_ref[2 * chunk, 0:CAP, :] = rows[:CAP]
        out_ref[2 * chunk + 1, 0:CAP, :] = rows[CAP:]
        both = pl.ds(2 * chunk, 2)
        leaving.append(
            pltpu.make_async_copy(out_ref.at[both], out_hbm.at[both], out_sems.at[chunk])
        )
        leaving[-1].start()
    for copy in leaving:
        copy.wait()


def column_of(row):
    return jnp.broadcast_to(row, (LANES, LANES)).T


def prep_kernel(col_ref, tgt_ref, ccol_ref, patch_ref):
    for t in range(col_ref.shape[1] // LANES):
        ccol_ref[t * LANES : (t + 1) * LANES, :] = column_of(
            col_ref[:, t * LANES : (t + 1) * LANES]
        )
    coef = column_of(tgt_ref[...])
    place = iota((LANES, LANES), 0)
    field = (place == iota((LANES, LANES), 1)).astype(F32)
    first = place % PATCH_ROW == 0
    last = place % PATCH_ROW == PATCH_ROW - 1
    zeros = jnp.zeros((PATCH_ROW, LANES), F32)
    for _ in range(HEAT_STEPS):
        west = jnp.where(first, 0.0, pltpu.roll(field, 1, 0))
        east = jnp.where(last, 0.0, pltpu.roll(field, LANES - 1, 0))
        north = jnp.concatenate([zeros, field[: LANES - PATCH_ROW]], axis=0)
        south = jnp.concatenate([field[PATCH_ROW:], zeros], axis=0)
        field = field + coef * (west + east + north + south - 4.0 * field)
    patch_ref[...] = field


def gather_kernel(msg_ref, ccol_ref, rcoef_ref, out_ref, onehot_ref, a_ref, b_ref):
    tiles = msg_ref.shape[0]
    cells = ccol_ref.shape[0]
    meta = msg_ref[:, CAP : CAP + META, :].astype(F32)
    weight = jnp.concatenate([meta[t, 0:1, :] for t in range(tiles)], axis=1)
    high = jnp.concatenate([meta[t, 1:2, :] for t in range(tiles)], axis=1)
    low = jnp.concatenate([meta[t, 2:3, :] for t in range(tiles)], axis=1)
    cell = high * 32.0 + low
    slots = tiles * CAP
    rows = msg_ref[:, 0:CAP, :].reshape(slots, LANES)
    pad = jnp.zeros((8, LANES), F32)
    for ref in (a_ref, b_ref):
        ref[0:8, :] = pad
        ref[8 + cells : 16 + cells, :] = pad
    for chunk in range(cells // 256):
        onehot_ref[...] = onehot_rows(cell, chunk * 256, 256)
        a_ref[8 + 256 * chunk : 8 + 256 * (chunk + 1), :] = jnp.dot(
            onehot_ref[...], rows, preferred_element_type=F32
        )
    blocks = cells // PATCH_ROW
    lane_shift = (lax.rem(lax.axis_index("tile"), 4) * 32).astype(F32)
    upper = jnp.where(iota((blocks, slots), 0).astype(F32) == high, weight, 0.0).astype(BF16)
    lower = (iota((LANES, slots), 0).astype(F32) == low + lane_shift).astype(F32).astype(BF16)
    mass = lax.dot_general(upper, lower, NT, preferred_element_type=F32)

    def step(src, dst):
        size = 128
        for c in range(cells // size):
            o = 8 + c * size
            mid = src[o : o + size, :]
            beside = src[o - 1 : o - 1 + size, :] + src[o + 1 : o + 1 + size, :]
            coef = ccol_ref[c * size : (c + 1) * size, :]
            dst[o : o + size, :] = mid + coef * (beside - 2.0 * mid)

    def two_steps(_, carry):
        step(a_ref, b_ref)
        step(b_ref, a_ref)
        return carry

    lax.fori_loop(0, HEAT_STEPS // 2, two_steps, 0)
    shift = lax.rem(lax.axis_index("tile") + 2, 4) * 32
    extra = mass + pltpu.roll(rcoef_ref[...], shift, 1)
    sub = iota((8, LANES), 0)
    for at in range(0, tiles * PART, 8):
        d, row = at // PART, at % PART
        start = 8 + 32 * d + row
        block = a_ref[start : start + 8, :]
        if row > 24:
            place = 32 - row
            after = a_ref[start - 1 : start + 7, :]
            block = jnp.where(
                sub < place, block, jnp.where(sub == place, extra[d : d + 1, :], after)
            )
        out_ref[at : at + 8, :] = block


def tile_of(parts):
    sub = iota((8, LANES), 0)
    out = jnp.broadcast_to(parts[0], (8, LANES))
    for t in range(1, 8):
        out = jnp.where(sub == t, parts[t], out)
    return out


def row_partials(kt_ref, vcol):
    parts = []
    for t in range(8):
        piece = kt_ref[:, t * LANES : (t + 1) * LANES].astype(F32)
        if vcol is not None:
            piece = piece * vcol
        parts.append(jnp.sum(piece, axis=0, keepdims=True))
    return tile_of(parts)


def band_kernel(
    msg_ref, patch_ref, weight_ref, kt_ref, short_ref, mass_ref, out_ref, coef_ref, field_ref
):
    tiles = msg_ref.shape[0] // PART
    owner = iota((8, LANES), 0) * 4 + iota((8, LANES), 1) // 32
    extra = [msg_ref[PART * r + 32 : PART * r + 33, :] for r in range(tiles)]
    mass = jnp.zeros((8, LANES), F32)
    coef = []
    for r in range(tiles):
        mass = jnp.where(owner == r, extra[r], mass)
    mass_ref[...] = mass
    for b in range(tiles // 8):
        coef.append(tile_of(extra[8 * b : 8 * b + 8]))
    coef.append(jnp.zeros((LANES - tiles, LANES), F32))
    coef = jnp.concatenate(coef, axis=0).T
    for r in range(tiles):
        at = 32 * ((r + 2) % 4)
        coef_ref[r, :, :] = jnp.broadcast_to(coef[at : at + 32, r : r + 1], (32, LANES))
    zero = jnp.zeros((8, LANES), F32)
    for b in range(4):
        place = slice(8 * b, 8 * b + 8)

        def step(_, field):
            out = []
            for r in range(tiles):
                up = field[r - 1] if r > 0 else zero
                down = field[r + 1] if r < tiles - 1 else zero
                out.append(field[r] + coef_ref[r, place, :] * (up + down - 2.0 * field[r]))
            return tuple(out)

        field = lax.fori_loop(
            0, HEAT_STEPS, step, tuple(msg_ref[PART * r + 8 * b : PART * r + 8 * b + 8, :] for r in range(tiles))
        )
        for r in range(tiles):
            field_ref[32 * r + 8 * b : 32 * r + 8 * b + 8, :] = field[r]
    smooth = lax.dot_general(
        patch_ref[...], field_ref[...], NT, preferred_element_type=F32, precision=EXACT
    )
    kernel = jnp.exp(EXPONENT_GAIN * smooth)
    kt_ref[...] = kernel
    short_ref[...] = kernel.astype(BF16)
    tile = row_partials(kt_ref, None)
    for g in range(out_ref.shape[0]):
        out_ref[g, 0:8, :] = tile
        out_ref[g, 8:16, :] = jnp.broadcast_to(weight_ref[...], (8, LANES))


def row_scale(msg_ref, mass_ref):
    total = msg_ref[0, 0:8, :]
    for g in range(1, msg_ref.shape[0]):
        total = total + msg_ref[g, 0:8, :]
    return mass_ref[...] / total


def scaled_columns(kt_ref, scale):
    pieces = [kt_ref[:, t * LANES : (t + 1) * LANES].astype(F32) for t in range(8)]
    return [piece * scale[t : t + 1, :] for t, piece in enumerate(pieces)]


def column_partials(kt_ref, scale):
    total = functools.reduce(lambda a, b: a + b, scaled_columns(kt_ref, scale))
    return jnp.sum(total.T, axis=0, keepdims=True)


def by_distance(msg_ref):
    groups = msg_ref.shape[0]
    me = lax.axis_index("grp")
    return tile_of([msg_ref[lax.rem(me + groups - k, groups), 8:9, :] for k in range(groups)])


def row_kernel(msg_ref, mass_ref, kt_ref, out_ref, weights_ref):
    weights_ref[...] = by_distance(msg_ref)
    column = column_partials(kt_ref, row_scale(msg_ref, mass_ref))
    for t in range(out_ref.shape[0]):
        out_ref[t, :, :] = column


def send_wide(out_ref, kernel_refs, scale):
    tile = tile_of([column_partials(ref, scale) for ref in kernel_refs])
    for t in range(out_ref.shape[0]):
        out_ref[t, :, :] = tile


def choose_kernel(even_ref, odd_ref, out_ref):
    odd = lax.rem(lax.axis_index("tile"), 2)

    @pl.when(odd == 0)
    def _():
        out_ref[...] = even_ref[...]

    @pl.when(odd == 1)
    def _():
        out_ref[...] = odd_ref[...]


def wide_row_sums(scale, kernel_refs):
    total = jnp.zeros((8, LANES), F32)
    for k, ref in enumerate(kernel_refs):
        total = total + row_partials(ref, column_of(scale[k : k + 1, :]))
    return total


def wide_row_kernel(msg_ref, mass_ref, *refs):
    kernel_refs, out_ref, later_ref = refs[:-2], refs[-2], refs[-1]
    scale = row_scale(msg_ref, mass_ref)
    send_wide(out_ref, kernel_refs, scale)
    later_ref[...] = scale * wide_row_sums(by_distance(msg_ref), kernel_refs)


def wide_row_scale(msg_ref, later_ref, weights_ref, kernel_refs):
    scale = column_scale([msg_ref[t] for t in range(msg_ref.shape[0])], weights_ref[...])
    return later_ref[...] / wide_row_sums(scale, kernel_refs)


def wide_round_kernel(msg_ref, later_ref, weights_ref, *refs):
    scale = wide_row_scale(msg_ref, later_ref, weights_ref, refs[:-1])
    send_wide(refs[-1], refs[:-1], scale)


def column_scale(parts, weight):
    while len(parts) > 1:
        parts = [a + b for a, b in zip(parts[0::2], parts[1::2])]
    return weight / parts[0]


def column_kernel(msg_ref, weight_ref, kt_ref, out_ref):
    scale = column_scale([msg_ref[t] for t in range(msg_ref.shape[0])], weight_ref[...])
    tile = row_partials(kt_ref, column_of(scale))
    for g in range(out_ref.shape[0]):
        out_ref[g, 0:8, :] = tile
        out_ref[g, 8:16, :] = jnp.broadcast_to(scale, (8, LANES))


def last_round_kernel(msg_ref, later_ref, weights_ref, *refs):
    out_ref = refs[-1]
    scale = wide_row_scale(msg_ref, later_ref, weights_ref, refs[:-1])
    pieces = scaled_columns(refs[0], scale)
    column = jnp.zeros((1, LANES), F32)
    for t in range(8):
        turned = pieces[t].T
        column = column + jnp.sum(turned, axis=0, keepdims=True)
        for r in range(4):
            at = PART * (4 * t + r)
            out_ref[at : at + 32, :] = turned[32 * r : 32 * r + 32]
    for at in range(32, out_ref.shape[0], PART):
        out_ref[at : at + 1, :] = column


def plan_kernel(cell_count, msg_ref, weight_ref, out_ref):
    tiles = msg_ref.shape[0] // PART
    sums = [msg_ref[PART * t + 32 : PART * t + 33, :] for t in range(tiles)]
    scale = column_scale(sums, weight_ref[...]) * cell_count
    for d in range(tiles):
        out_ref[0, 32 * d : 32 * d + 32, :] = msg_ref[PART * d : PART * d + 32, :] * scale


def swap(values, axis):
    return lax.all_to_all(values, axis, split_axis=0, concat_axis=0, tiled=True)


def swap_parts(parts, axis):
    size = lax.axis_size(axis)
    return swap(parts.reshape(size, PART, 1, LANES), axis).reshape(size * PART, LANES)


def body(spot_terms, spot_weight, spot_owner, spot_cell, col_coef, row_coef, tgt_coef, tgt_weight):
    tiles = lax.axis_size("tile")
    groups = lax.axis_size("grp")
    spots, columns = spot_terms.shape
    cells = col_coef.shape[1]
    shape = jax.ShapeDtypeStruct
    weight = tgt_weight.reshape(1, columns)

    packed = call(
        pack_kernel,
        shape((tiles, CAP + META, columns), BF16),
        [
            spot_owner.reshape(1, spots),
            spot_cell.reshape(1, spots),
            spot_weight.reshape(spots // LANES, LANES),
            spot_terms,
        ],
        scratch=[
            pltpu.VMEM((tiles, CAP + META, columns), BF16),
            pltpu.VMEM((256, spots), BF16),
            pltpu.VMEM((1, spots), jnp.int32),
            pltpu.VMEM((1, spots), jnp.int32),
            pltpu.VMEM((spots // LANES, LANES), BF16),
            pltpu.VMEM((spots, columns), BF16),
            pltpu.SemaphoreType.DMA((4,)),
            pltpu.SemaphoreType.DMA((tiles * CAP // 256,)),
        ],
        hbm=(0, 1, 2, 3),
        out_hbm=True,
    )
    ccol, patch = call(
        prep_kernel,
        (shape((cells, LANES), F32), shape((LANES, LANES), F32)),
        [col_coef, tgt_coef.reshape(1, columns)],
    )
    rcoef = jnp.pad(row_coef.reshape(tiles, 32), ((0, 0), (0, LANES - 32)))
    got = swap(packed, "tile")
    sorted_field = call(
        gather_kernel,
        shape((tiles * PART, LANES), F32),
        [got, ccol, rcoef],
        scratch=[
            pltpu.VMEM((256, tiles * CAP), BF16),
            pltpu.VMEM((cells + 16, LANES), F32),
            pltpu.VMEM((cells + 16, LANES), F32),
        ],
    )
    band = swap_parts(sorted_field, "tile")
    tile = shape((8, LANES), F32)
    wide = shape((tiles, groups, LANES), F32)
    field = (columns, cells)
    kt, short, mass, rows = call(
        band_kernel,
        (shape(field, F32), shape(field, BF16), tile, shape((groups, 16, LANES), F32)),
        [band, patch, weight],
        scratch=[pltpu.VMEM((tiles, 32, LANES), F32), pltpu.VMEM((cells, LANES), F32)],
    )
    up = [(g, (g + 1) % groups) for g in range(groups)]
    down = [(g, (g - 1) % groups) for g in range(groups)]
    before = [kt, lax.ppermute(short, "grp", up)]
    after = [kt, lax.ppermute(short, "grp", down)]


    def forward(value):
        value, last, first = lax.optimization_barrier((value, before[-1], after[-1]))
        before[-1], after[-1] = last, first
        before.append(lax.ppermute(last, "grp", up))
        after.append(lax.ppermute(first, "grp", down))
        return value

    rows = forward(swap(rows, "grp"))
    leap = [
        (g * tiles + t, (g - 3 + 6 * (t % 2)) % groups * tiles + t)
        for g in range(groups)
        for t in range(tiles)
    ]
    opposite = call(choose_kernel, shape(field, BF16), [after[1], before[1]])
    opposite = lax.ppermute(opposite, ("grp", "tile"), leap)
    cols, weights = call(row_kernel, (shape((tiles, 1, LANES), F32), tile), [rows, mass, kt])
    cols = forward(swap(cols, "tile"))
    rows = call(column_kernel, shape((groups, 16, LANES), F32), [cols, weight, kt])
    rows, opposite = lax.optimization_barrier((rows, opposite))
    rows = swap(rows, "grp")
    every = before + [opposite] + after[:0:-1]
    cols, later = call(wide_row_kernel, (wide, tile), [rows, mass] + every)
    for _ in range(SCALING_ROUNDS - 3):
        cols = swap(cols, "tile")
        cols = call(wide_round_kernel, wide, [cols, later, weights] + every)
    cols = swap(cols, "tile")
    scaled = call(
        last_round_kernel, shape((tiles * PART, LANES), F32), [cols, later, weights] + every
    )
    scaled = swap_parts(scaled, "tile")
    return call(
        functools.partial(plan_kernel, float(cells * tiles)),
        shape((1, cells, LANES), F32),
        [scaled, weight],
    )


def solution(mesh):
    return jax.shard_map(
        body,
        mesh=mesh,
        in_specs=(
            P("tile", "grp"),
            P("tile"),
            P("tile", None),
            P("tile"),
            P("tile", None),
            P("tile", None),
            P("grp"),
            P("grp"),
        ),
        out_specs=P("tile", None, "grp"),
        check_vma=False,
    )
```

```python
import functools

import jax
import jax.numpy as jnp
from jax import lax
from jax.experimental import pallas as pl
from jax.experimental.pallas import tpu as pltpu
from jax.sharding import PartitionSpec as P

PATCH_ROW = 32
HEAT_STEPS = 10
SCALING_ROUNDS = 5
EXPONENT_GAIN = 2.0
LANES = 128
CAP = 128
META = 16
PART = 33
F32 = jnp.float32
BF16 = jnp.bfloat16
NT = (((1,), (1,)), ((), ()))
EXACT = lax.Precision.HIGHEST


def iota(shape, axis):
    return lax.broadcasted_iota(jnp.int32, shape, axis)


def call(kernel, out_shape, operands, scratch=(), hbm=(), out_hbm=False):
    specs = []
    for i in range(len(operands)):
        space = pltpu.HBM if i in hbm else pltpu.VMEM
        specs.append(pl.BlockSpec(memory_space=space))
    out_space = pltpu.HBM if out_hbm else pltpu.VMEM
    outs = jax.tree.map(lambda _: pl.BlockSpec(memory_space=out_space), out_shape)
    return pl.pallas_call(
        kernel,
        out_shape=out_shape,
        in_specs=specs,
        out_specs=outs,
        scratch_shapes=list(scratch),
        compiler_params=pltpu.CompilerParams(vmem_limit_bytes=(60 if hbm else 40) * 2**20),
    )(*operands)


def onehot_rows(index, base, rows):
    n = index.shape[1]
    local = jnp.clip(index - float(base), -1.0, float(rows))
    local = jnp.broadcast_to(local, (16, n)).astype(BF16)
    row = iota((rows, LANES), 0).astype(F32).astype(BF16)
    row = row.reshape(rows // 16, 16, LANES)
    one = jnp.ones((rows // 16, 16, LANES), BF16)
    zero = jnp.zeros((rows // 16, 16, LANES), BF16)
    pieces = []
    for j in range(n // LANES):
        piece = local[None, :, j * LANES : (j + 1) * LANES]
        piece = jnp.broadcast_to(piece, row.shape)
        pieces.append(jnp.where(row == piece, one, zero).reshape(rows, LANES))
    return jnp.concatenate(pieces, axis=1)


def pack_kernel(
    owner_hbm, cell_hbm, weight_hbm, terms_hbm, out_hbm,
    out_ref, onehot_ref, owner_ref, cell_ref, weight_ref, terms_ref, sems, out_sems,
):
    tiles = out_ref.shape[0]
    spots = terms_ref.shape[0]
    block = 256
    pairs = [
        (owner_hbm, owner_ref), (cell_hbm, cell_ref), (weight_hbm, weight_ref), (terms_hbm, terms_ref),
    ]
    copies = [pltpu.make_async_copy(src, dst, sems.at[i]) for i, (src, dst) in enumerate(pairs)]
    for copy in copies:
        copy.start()
    before = (iota((block, block), 0) < iota((block, block), 1)).astype(F32).astype(BF16)
    copies[0].wait()
    owner = owner_ref[...]
    base = jnp.zeros((tiles, 1), F32)
    ranks = []
    for b in range(spots // block):
        own = owner[:, b * block : (b + 1) * block]
        member = (iota((tiles, block), 0) == own).astype(F32)
        inside = jnp.dot(member.astype(BF16), before, preferred_element_type=F32)
        ranks.append(jnp.sum(member * (inside + base), axis=0, keepdims=True))
        base = base + inside[:, block - 1 : block] + member[:, block - 1 : block]
    rank = jnp.concatenate(ranks, axis=1)
    slot = owner.astype(F32) * float(CAP) + rank
    for copy in copies[1:]:
        copy.wait()
    cell = cell_ref[...]
    high = (cell // 32).astype(F32)
    low = (cell % 32).astype(F32)
    weight = weight_ref[...].astype(F32)
    weight = jnp.concatenate([weight[i : i + 1] for i in range(spots // LANES)], axis=1)
    which = iota((tiles * 8, spots), 0)
    kind = which % 8
    value = jnp.where(kind == 0, weight, jnp.where(kind == 1, high, jnp.where(kind == 2, low, 0.0)))
    value = jnp.where(which // 8 == owner, value, 0.0).astype(BF16)
    onehot_ref[0:CAP, :] = onehot_rows(rank, 0, CAP)
    meta = lax.dot_general(value, onehot_ref[0:CAP, :], NT, preferred_element_type=F32)
    empty = jnp.zeros((8, LANES), F32)
    for t in range(tiles):
        out_ref[t, CAP : CAP + META, :] = jnp.concatenate(
            [meta[8 * t : 8 * t + 8], empty], axis=0
        ).astype(BF16)
    terms = terms_ref[...]
    leaving = []
    for chunk in range(tiles * CAP // 256):
        onehot_ref[...] = onehot_rows(slot, chunk * 256, 256)
        rows = jnp.dot(onehot_ref[...], terms, preferred_element_type=F32).astype(BF16)
        out_ref[2 * chunk, 0:CAP, :] = rows[:CAP]
        out_ref[2 * chunk + 1, 0:CAP, :] = rows[CAP:]
        both = pl.ds(2 * chunk, 2)
        leaving.append(
            pltpu.make_async_copy(out_ref.at[both], out_hbm.at[both], out_sems.at[chunk])
        )
        leaving[-1].start()
    for copy in leaving:
        copy.wait()


def column_of(row):
    return jnp.broadcast_to(row, (LANES, LANES)).T


def prep_kernel(col_ref, tgt_ref, ccol_ref, patch_ref):
    for t in range(col_ref.shape[1] // LANES):
        ccol_ref[t * LANES : (t + 1) * LANES, :] = column_of(
            col_ref[:, t * LANES : (t + 1) * LANES]
        )
    coef = column_of(tgt_ref[...])
    place = iota((LANES, LANES), 0)
    field = (place == iota((LANES, LANES), 1)).astype(F32)
    first = place % PATCH_ROW == 0
    last = place % PATCH_ROW == PATCH_ROW - 1
    zeros = jnp.zeros((PATCH_ROW, LANES), F32)
    for _ in range(HEAT_STEPS):
        west = jnp.where(first, 0.0, pltpu.roll(field, 1, 0))
        east = jnp.where(last, 0.0, pltpu.roll(field, LANES - 1, 0))
        north = jnp.concatenate([zeros, field[: LANES - PATCH_ROW]], axis=0)
        south = jnp.concatenate([field[PATCH_ROW:], zeros], axis=0)
        field = field + coef * (west + east + north + south - 4.0 * field)
    patch_ref[...] = field


def gather_kernel(msg_ref, ccol_ref, rcoef_ref, out_ref, onehot_ref, a_ref, b_ref):
    tiles = msg_ref.shape[0]
    cells = ccol_ref.shape[0]
    meta = msg_ref[:, CAP : CAP + META, :].astype(F32)
    weight = jnp.concatenate([meta[t, 0:1, :] for t in range(tiles)], axis=1)
    high = jnp.concatenate([meta[t, 1:2, :] for t in range(tiles)], axis=1)
    low = jnp.concatenate([meta[t, 2:3, :] for t in range(tiles)], axis=1)
    cell = high * 32.0 + low
    slots = tiles * CAP
    rows = msg_ref[:, 0:CAP, :].reshape(slots, LANES)
    pad = jnp.zeros((8, LANES), F32)
    for ref in (a_ref, b_ref):
        ref[0:8, :] = pad
        ref[8 + cells : 16 + cells, :] = pad
    for chunk in range(cells // 256):
        onehot_ref[...] = onehot_rows(cell, chunk * 256, 256)
        a_ref[8 + 256 * chunk : 8 + 256 * (chunk + 1), :] = jnp.dot(
            onehot_ref[...], rows, preferred_element_type=F32
        )
    blocks = cells // PATCH_ROW
    lane_shift = (lax.rem(lax.axis_index("tile"), 4) * 32).astype(F32)
    upper = jnp.where(iota((blocks, slots), 0).astype(F32) == high, weight, 0.0).astype(BF16)
    lower = (iota((LANES, slots), 0).astype(F32) == low + lane_shift).astype(F32).astype(BF16)
    mass = lax.dot_general(upper, lower, NT, preferred_element_type=F32)

    def step(src, dst):
        size = 128
        for c in range(cells // size):
            o = 8 + c * size
            mid = src[o : o + size, :]
            beside = src[o - 1 : o - 1 + size, :] + src[o + 1 : o + 1 + size, :]
            coef = ccol_ref[c * size : (c + 1) * size, :]
            dst[o : o + size, :] = mid + coef * (beside - 2.0 * mid)

    def two_steps(_, carry):
        step(a_ref, b_ref)
        step(b_ref, a_ref)
        return carry

    lax.fori_loop(0, HEAT_STEPS // 2, two_steps, 0)
    quarter = lax.rem(lax.axis_index("tile"), 4)
    extra = jnp.where(iota((tiles, LANES), 1) // 32 == quarter, mass, rcoef_ref[...])
    sub = iota((8, LANES), 0)
    for at in range(0, tiles * PART, 8):
        d, row = at // PART, at % PART
        start = 8 + 32 * d + row
        block = a_ref[start : start + 8, :]
        if row > 24:
            place = 32 - row
            after = a_ref[start - 1 : start + 7, :]
            block = jnp.where(
                sub < place, block, jnp.where(sub == place, extra[d : d + 1, :], after)
            )
        out_ref[at : at + 8, :] = block


def tile_of(parts):
    sub = iota((8, LANES), 0)
    out = jnp.broadcast_to(parts[0], (8, LANES))
    for t in range(1, 8):
        out = jnp.where(sub == t, parts[t], out)
    return out


def row_partials(kt_ref, vcol):
    parts = []
    for t in range(8):
        piece = kt_ref[:, t * LANES : (t + 1) * LANES].astype(F32)
        if vcol is not None:
            piece = piece * vcol
        parts.append(jnp.sum(piece, axis=0, keepdims=True))
    return tile_of(parts)


def band_kernel(
    msg_ref, patch_ref, weight_ref, kt_ref, short_ref, mass_ref, out_ref, coef_ref, field_ref
):
    tiles = msg_ref.shape[0] // PART
    owner = iota((8, LANES), 0) * 4 + iota((8, LANES), 1) // 32
    extra = [msg_ref[PART * r + 32 : PART * r + 33, :] for r in range(tiles)]
    mass = jnp.zeros((8, LANES), F32)
    coef = []
    for r in range(tiles):
        mass = jnp.where(owner == r, extra[r], mass)
    mass_ref[...] = mass
    for b in range(tiles // 8):
        coef.append(tile_of(extra[8 * b : 8 * b + 8]))
    coef.append(jnp.zeros((LANES - tiles, LANES), F32))
    coef = jnp.concatenate(coef, axis=0).T
    for r in range(tiles):
        at = 32 * ((r + 2) % 4)
        coef_ref[r, :, :] = jnp.broadcast_to(coef[at : at + 32, r : r + 1], (32, LANES))
    zero = jnp.zeros((8, LANES), F32)
    for b in range(4):
        place = slice(8 * b, 8 * b + 8)

        def step(_, field):
            out = []
            for r in range(tiles):
                up = field[r - 1] if r > 0 else zero
                down = field[r + 1] if r < tiles - 1 else zero
                out.append(field[r] + coef_ref[r, place, :] * (up + down - 2.0 * field[r]))
            return tuple(out)

        field = lax.fori_loop(
            0, HEAT_STEPS, step, tuple(msg_ref[PART * r + 8 * b : PART * r + 8 * b + 8, :] for r in range(tiles))
        )
        for r in range(tiles):
            field_ref[32 * r + 8 * b : 32 * r + 8 * b + 8, :] = field[r]
    smooth = lax.dot_general(
        patch_ref[...], field_ref[...], NT, preferred_element_type=F32, precision=EXACT
    )
    kernel = jnp.exp(EXPONENT_GAIN * smooth)
    kt_ref[...] = kernel
    short_ref[...] = kernel.astype(BF16)
    tile = row_partials(kt_ref, None)
    for g in range(out_ref.shape[0]):
        out_ref[g, 0:8, :] = tile
        out_ref[g, 8:16, :] = jnp.broadcast_to(weight_ref[...], (8, LANES))


def row_scale(msg_ref, mass_ref):
    total = msg_ref[0, 0:8, :]
    for g in range(1, msg_ref.shape[0]):
        total = total + msg_ref[g, 0:8, :]
    return mass_ref[...] / total


def scaled_columns(kt_ref, scale):
    pieces = [kt_ref[:, t * LANES : (t + 1) * LANES].astype(F32) for t in range(8)]
    return [piece * scale[t : t + 1, :] for t, piece in enumerate(pieces)]


def column_partials(kt_ref, scale):
    total = functools.reduce(lambda a, b: a + b, scaled_columns(kt_ref, scale))
    return jnp.sum(total.T, axis=0, keepdims=True)


def by_distance(msg_ref):
    groups = msg_ref.shape[0]
    me = lax.axis_index("grp")
    return tile_of([msg_ref[lax.rem(me + groups - k, groups), 8:9, :] for k in range(groups)])


def row_kernel(msg_ref, mass_ref, kt_ref, out_ref, weights_ref):
    weights_ref[...] = by_distance(msg_ref)
    column = column_partials(kt_ref, row_scale(msg_ref, mass_ref))
    for t in range(out_ref.shape[0]):
        out_ref[t, :, :] = column


def send_wide(out_ref, kernel_refs, scale):
    tile = tile_of([column_partials(ref, scale) for ref in kernel_refs])
    for t in range(out_ref.shape[0]):
        out_ref[t, :, :] = tile


def choose_kernel(even_ref, odd_ref, out_ref):
    odd = lax.rem(lax.axis_index("tile"), 2)

    @pl.when(odd == 0)
    def _():
        out_ref[...] = even_ref[...]

    @pl.when(odd == 1)
    def _():
        out_ref[...] = odd_ref[...]


def wide_row_sums(scale, kernel_refs):
    total = jnp.zeros((8, LANES), F32)
    for k, ref in enumerate(kernel_refs):
        total = total + row_partials(ref, column_of(scale[k : k + 1, :]))
    return total


def wide_row_kernel(msg_ref, mass_ref, *refs):
    kernel_refs, out_ref, later_ref = refs[:-2], refs[-2], refs[-1]
    scale = row_scale(msg_ref, mass_ref)
    send_wide(out_ref, kernel_refs, scale)
    later_ref[...] = scale * wide_row_sums(by_distance(msg_ref), kernel_refs)


def wide_row_scale(msg_ref, later_ref, weights_ref, kernel_refs):
    scale = column_scale([msg_ref[t] for t in range(msg_ref.shape[0])], weights_ref[...])
    return later_ref[...] / wide_row_sums(scale, kernel_refs)


def wide_round_kernel(msg_ref, later_ref, weights_ref, *refs):
    scale = wide_row_scale(msg_ref, later_ref, weights_ref, refs[:-1])
    send_wide(refs[-1], refs[:-1], scale)


def column_scale(parts, weight):
    while len(parts) > 1:
        parts = [a + b for a, b in zip(parts[0::2], parts[1::2])]
    return weight / parts[0]


def column_kernel(msg_ref, weight_ref, kt_ref, out_ref):
    scale = column_scale([msg_ref[t] for t in range(msg_ref.shape[0])], weight_ref[...])
    tile = row_partials(kt_ref, column_of(scale))
    for g in range(out_ref.shape[0]):
        out_ref[g, 0:8, :] = tile
        out_ref[g, 8:16, :] = jnp.broadcast_to(scale, (8, LANES))


def last_round_kernel(msg_ref, later_ref, weights_ref, *refs):
    out_ref = refs[-1]
    scale = wide_row_scale(msg_ref, later_ref, weights_ref, refs[:-1])
    pieces = scaled_columns(refs[0], scale)
    column = jnp.zeros((1, LANES), F32)
    for t in range(8):
        turned = pieces[t].T
        column = column + jnp.sum(turned, axis=0, keepdims=True)
        for r in range(4):
            at = PART * (4 * t + r)
            out_ref[at : at + 32, :] = turned[32 * r : 32 * r + 32]
    for at in range(32, out_ref.shape[0], PART):
        out_ref[at : at + 1, :] = column


def plan_kernel(cell_count, msg_ref, weight_ref, out_ref):
    tiles = msg_ref.shape[0] // PART
    sums = [msg_ref[PART * t + 32 : PART * t + 33, :] for t in range(tiles)]
    scale = column_scale(sums, weight_ref[...]) * cell_count
    for d in range(tiles):
        out_ref[0, 32 * d : 32 * d + 32, :] = msg_ref[PART * d : PART * d + 32, :] * scale


def swap(values, axis):
    return lax.all_to_all(values, axis, split_axis=0, concat_axis=0, tiled=True)


def swap_parts(parts, axis):
    size = lax.axis_size(axis)
    return swap(parts.reshape(size, PART, 1, LANES), axis).reshape(size * PART, LANES)


def body(spot_terms, spot_weight, spot_owner, spot_cell, col_coef, row_coef, tgt_coef, tgt_weight):
    tiles = lax.axis_size("tile")
    groups = lax.axis_size("grp")
    spots, columns = spot_terms.shape
    cells = col_coef.shape[1]
    shape = jax.ShapeDtypeStruct
    weight = tgt_weight.reshape(1, columns)

    packed = call(
        pack_kernel,
        shape((tiles, CAP + META, columns), BF16),
        [
            spot_owner.reshape(1, spots),
            spot_cell.reshape(1, spots),
            spot_weight.reshape(spots // LANES, LANES),
            spot_terms,
        ],
        scratch=[
            pltpu.VMEM((tiles, CAP + META, columns), BF16),
            pltpu.VMEM((256, spots), BF16),
            pltpu.VMEM((1, spots), jnp.int32),
            pltpu.VMEM((1, spots), jnp.int32),
            pltpu.VMEM((spots // LANES, LANES), BF16),
            pltpu.VMEM((spots, columns), BF16),
            pltpu.SemaphoreType.DMA((4,)),
            pltpu.SemaphoreType.DMA((tiles * CAP // 256,)),
        ],
        hbm=(0, 1, 2, 3),
        out_hbm=True,
    )
    ccol, patch = call(
        prep_kernel,
        (shape((cells, LANES), F32), shape((LANES, LANES), F32)),
        [col_coef, tgt_coef.reshape(1, columns)],
    )
    rcoef = jnp.tile(row_coef.reshape(tiles, 32), (1, LANES // 32))
    got = swap(packed, "tile")
    sorted_field = call(
        gather_kernel,
        shape((tiles * PART, LANES), F32),
        [got, ccol, rcoef],
        scratch=[
            pltpu.VMEM((256, tiles * CAP), BF16),
            pltpu.VMEM((cells + 16, LANES), F32),
            pltpu.VMEM((cells + 16, LANES), F32),
        ],
    )
    band = swap_parts(sorted_field, "tile")
    tile = shape((8, LANES), F32)
    wide = shape((tiles, groups, LANES), F32)
    field = (columns, cells)
    kt, short, mass, rows = call(
        band_kernel,
        (shape(field, F32), shape(field, BF16), tile, shape((groups, 16, LANES), F32)),
        [band, patch, weight],
        scratch=[pltpu.VMEM((tiles, 32, LANES), F32), pltpu.VMEM((cells, LANES), F32)],
    )
    up = [(g, (g + 1) % groups) for g in range(groups)]
    down = [(g, (g - 1) % groups) for g in range(groups)]
    before = [kt, lax.ppermute(short, "grp", up)]
    after = [kt, lax.ppermute(short, "grp", down)]


    def forward(value):
        value, last, first = lax.optimization_barrier((value, before[-1], after[-1]))
        before[-1], after[-1] = last, first
        before.append(lax.ppermute(last, "grp", up))
        after.append(lax.ppermute(first, "grp", down))
        return value

    rows = forward(swap(rows, "grp"))
    leap = [
        (g * tiles + t, (g - 3 + 6 * (t % 2)) % groups * tiles + t)
        for g in range(groups)
        for t in range(tiles)
    ]
    opposite = call(choose_kernel, shape(field, BF16), [after[1], before[1]])
    opposite = lax.ppermute(opposite, ("grp", "tile"), leap)
    cols, weights = call(row_kernel, (shape((tiles, 1, LANES), F32), tile), [rows, mass, kt])
    cols = forward(swap(cols, "tile"))
    rows = call(column_kernel, shape((groups, 16, LANES), F32), [cols, weight, kt])
    rows, opposite = lax.optimization_barrier((rows, opposite))
    rows = swap(rows, "grp")
    every = before + [opposite] + after[:0:-1]
    cols, later = call(wide_row_kernel, (wide, tile), [rows, mass] + every)
    for _ in range(SCALING_ROUNDS - 3):
        cols = swap(cols, "tile")
        cols = call(wide_round_kernel, wide, [cols, later, weights] + every)
    cols = swap(cols, "tile")
    scaled = call(
        last_round_kernel, shape((tiles * PART, LANES), F32), [cols, later, weights] + every
    )
    scaled = swap_parts(scaled, "tile")
    return call(
        functools.partial(plan_kernel, float(cells * tiles)),
        shape((1, cells, LANES), F32),
        [scaled, weight],
    )


def solution(mesh):
    return jax.shard_map(
        body,
        mesh=mesh,
        in_specs=(
            P("tile", "grp"),
            P("tile"),
            P("tile", None),
            P("tile"),
            P("tile", None),
            P("tile", None),
            P("grp"),
            P("grp"),
        ),
        out_specs=P("tile", None, "grp"),
        check_vma=False,
    )
```

```python
import functools

import jax
import jax.numpy as jnp
from jax import lax
from jax.experimental import pallas as pl
from jax.experimental.pallas import tpu as pltpu
from jax.sharding import PartitionSpec as P

PATCH_ROW = 32
HEAT_STEPS = 10
SCALING_ROUNDS = 5
EXPONENT_GAIN = 2.0
LANES = 128
CAP = 128
META = 16
PART = 33
F32 = jnp.float32
BF16 = jnp.bfloat16
BF16_MAX = float(jnp.finfo(jnp.bfloat16).max)
NT = (((1,), (1,)), ((), ()))
EXACT = lax.Precision.HIGHEST


def iota(shape, axis):
    return lax.broadcasted_iota(jnp.int32, shape, axis)


def call(kernel, out_shape, operands, scratch=(), hbm=(), out_hbm=False):
    specs = []
    for i in range(len(operands)):
        space = pltpu.HBM if i in hbm else pltpu.VMEM
        specs.append(pl.BlockSpec(memory_space=space))
    out_space = pltpu.HBM if out_hbm else pltpu.VMEM
    outs = jax.tree.map(lambda _: pl.BlockSpec(memory_space=out_space), out_shape)
    return pl.pallas_call(
        kernel,
        out_shape=out_shape,
        in_specs=specs,
        out_specs=outs,
        scratch_shapes=list(scratch),
        compiler_params=pltpu.CompilerParams(vmem_limit_bytes=(60 if hbm else 40) * 2**20),
    )(*operands)


def onehot_rows(index, base, rows):
    n = index.shape[1]
    local = jnp.clip(index - float(base), -1.0, float(rows))
    local = jnp.broadcast_to(local, (16, n)).astype(BF16)
    row = iota((rows, LANES), 0).astype(F32).astype(BF16)
    row = row.reshape(rows // 16, 16, LANES)
    one = jnp.ones((rows // 16, 16, LANES), BF16)
    zero = jnp.zeros((rows // 16, 16, LANES), BF16)
    pieces = []
    for j in range(n // LANES):
        piece = local[None, :, j * LANES : (j + 1) * LANES]
        piece = jnp.broadcast_to(piece, row.shape)
        pieces.append(jnp.where(row == piece, one, zero).reshape(rows, LANES))
    return jnp.concatenate(pieces, axis=1)


def pack_kernel(
    owner_hbm, cell_hbm, weight_hbm, terms_hbm, out_hbm,
    out_ref, onehot_ref, owner_ref, cell_ref, weight_ref, terms_ref, sems, out_sems,
):
    tiles = out_ref.shape[0]
    spots = terms_ref.shape[0]
    block = 256
    pairs = [
        (owner_hbm, owner_ref), (cell_hbm, cell_ref), (weight_hbm, weight_ref), (terms_hbm, terms_ref),
    ]
    copies = [pltpu.make_async_copy(src, dst, sems.at[i]) for i, (src, dst) in enumerate(pairs)]
    for copy in copies:
        copy.start()
    before = (iota((block, block), 0) < iota((block, block), 1)).astype(F32).astype(BF16)
    copies[0].wait()
    owner = owner_ref[...]
    base = jnp.zeros((tiles, 1), F32)
    ranks = []
    for b in range(spots // block):
        own = owner[:, b * block : (b + 1) * block]
        member = (iota((tiles, block), 0) == own).astype(F32)
        inside = jnp.dot(member.astype(BF16), before, preferred_element_type=F32)
        ranks.append(jnp.sum(member * (inside + base), axis=0, keepdims=True))
        base = base + inside[:, block - 1 : block] + member[:, block - 1 : block]
    rank = jnp.concatenate(ranks, axis=1)
    slot = owner.astype(F32) * float(CAP) + rank
    for copy in copies[1:]:
        copy.wait()
    cell = cell_ref[...]
    high = (cell // 32).astype(F32)
    low = (cell % 32).astype(F32)
    weight = weight_ref[...].astype(F32)
    weight = jnp.concatenate([weight[i : i + 1] for i in range(spots // LANES)], axis=1)
    which = iota((tiles * 8, spots), 0)
    kind = which % 8
    value = jnp.where(kind == 0, weight, jnp.where(kind == 1, high, jnp.where(kind == 2, low, 0.0)))
    value = jnp.where(which // 8 == owner, value, 0.0).astype(BF16)
    onehot_ref[0:CAP, :] = onehot_rows(rank, 0, CAP)
    meta = lax.dot_general(value, onehot_ref[0:CAP, :], NT, preferred_element_type=F32)
    empty = jnp.zeros((8, LANES), F32)
    for t in range(tiles):
        out_ref[t, CAP : CAP + META, :] = jnp.concatenate(
            [meta[8 * t : 8 * t + 8], empty], axis=0
        ).astype(BF16)
    terms = terms_ref[...]
    leaving = []
    for chunk in range(tiles * CAP // 256):
        onehot_ref[...] = onehot_rows(slot, chunk * 256, 256)
        rows = jnp.dot(onehot_ref[...], terms, preferred_element_type=F32).astype(BF16)
        out_ref[2 * chunk, 0:CAP, :] = rows[:CAP]
        out_ref[2 * chunk + 1, 0:CAP, :] = rows[CAP:]
        both = pl.ds(2 * chunk, 2)
        leaving.append(
            pltpu.make_async_copy(out_ref.at[both], out_hbm.at[both], out_sems.at[chunk])
        )
        leaving[-1].start()
    for copy in leaving:
        copy.wait()


def column_of(row):
    return jnp.broadcast_to(row, (LANES, LANES)).T


def prep_kernel(col_ref, tgt_ref, ccol_ref, patch_ref):
    for t in range(col_ref.shape[1] // LANES):
        ccol_ref[t * LANES : (t + 1) * LANES, :] = column_of(
            col_ref[:, t * LANES : (t + 1) * LANES]
        )
    coef = column_of(tgt_ref[...])
    place = iota((LANES, LANES), 0)
    field = (place == iota((LANES, LANES), 1)).astype(F32)
    first = place % PATCH_ROW == 0
    last = place % PATCH_ROW == PATCH_ROW - 1
    zeros = jnp.zeros((PATCH_ROW, LANES), F32)
    for _ in range(HEAT_STEPS):
        west = jnp.where(first, 0.0, pltpu.roll(field, 1, 0))
        east = jnp.where(last, 0.0, pltpu.roll(field, LANES - 1, 0))
        north = jnp.concatenate([zeros, field[: LANES - PATCH_ROW]], axis=0)
        south = jnp.concatenate([field[PATCH_ROW:], zeros], axis=0)
        field = field + coef * (west + east + north + south - 4.0 * field)
    patch_ref[...] = field


def gather_kernel(msg_ref, ccol_ref, rcoef_ref, out_ref, onehot_ref, a_ref, b_ref):
    tiles = msg_ref.shape[0]
    cells = ccol_ref.shape[0]
    meta = msg_ref[:, CAP : CAP + META, :].astype(F32)
    weight = jnp.concatenate([meta[t, 0:1, :] for t in range(tiles)], axis=1)
    high = jnp.concatenate([meta[t, 1:2, :] for t in range(tiles)], axis=1)
    low = jnp.concatenate([meta[t, 2:3, :] for t in range(tiles)], axis=1)
    cell = high * 32.0 + low
    slots = tiles * CAP
    rows = msg_ref[:, 0:CAP, :].reshape(slots, LANES)
    pad = jnp.zeros((8, LANES), F32)
    for ref in (a_ref, b_ref):
        ref[0:8, :] = pad
        ref[8 + cells : 16 + cells, :] = pad
    for chunk in range(cells // 256):
        onehot_ref[...] = onehot_rows(cell, chunk * 256, 256)
        a_ref[8 + 256 * chunk : 8 + 256 * (chunk + 1), :] = jnp.dot(
            onehot_ref[...], rows, preferred_element_type=F32
        )
    blocks = cells // PATCH_ROW
    lane_shift = (lax.rem(lax.axis_index("tile"), 4) * 32).astype(F32)
    upper = jnp.where(iota((blocks, slots), 0).astype(F32) == high, weight, 0.0).astype(BF16)
    lower = (iota((LANES, slots), 0).astype(F32) == low + lane_shift).astype(F32).astype(BF16)
    mass = lax.dot_general(upper, lower, NT, preferred_element_type=F32)

    def step(src, dst):
        size = 128
        for c in range(cells // size):
            o = 8 + c * size
            mid = src[o : o + size, :]
            beside = src[o - 1 : o - 1 + size, :] + src[o + 1 : o + 1 + size, :]
            coef = ccol_ref[c * size : (c + 1) * size, :]
            dst[o : o + size, :] = mid + coef * (beside - 2.0 * mid)

    def two_steps(_, carry):
        step(a_ref, b_ref)
        step(b_ref, a_ref)
        return carry

    lax.fori_loop(0, HEAT_STEPS // 2, two_steps, 0)
    quarter = lax.rem(lax.axis_index("tile"), 4)
    extra = jnp.where(iota((tiles, LANES), 1) // 32 == quarter, mass, rcoef_ref[...])
    sub = iota((8, LANES), 0)
    for at in range(0, tiles * PART, 8):
        d, row = at // PART, at % PART
        start = 8 + 32 * d + row
        block = a_ref[start : start + 8, :]
        if row > 24:
            place = 32 - row
            after = a_ref[start - 1 : start + 7, :]
            block = jnp.where(
                sub < place, block, jnp.where(sub == place, extra[d : d + 1, :], after)
            )
        out_ref[at : at + 8, :] = block


def tile_of(parts):
    sub = iota((8, LANES), 0)
    out = jnp.broadcast_to(parts[0], (8, LANES))
    for t in range(1, 8):
        out = jnp.where(sub == t, parts[t], out)
    return out


def row_partials(kt_ref, vcol):
    parts = []
    for t in range(8):
        piece = kt_ref[:, t * LANES : (t + 1) * LANES].astype(F32)
        if vcol is not None:
            piece = piece * vcol
        parts.append(jnp.sum(piece, axis=0, keepdims=True))
    return tile_of(parts)


def band_kernel(
    msg_ref, patch_ref, weight_ref, kt_ref, short_ref, mass_ref, out_ref, coef_ref, field_ref
):
    tiles = msg_ref.shape[0] // PART
    owner = iota((8, LANES), 0) * 4 + iota((8, LANES), 1) // 32
    extra = [msg_ref[PART * r + 32 : PART * r + 33, :] for r in range(tiles)]
    mass = jnp.zeros((8, LANES), F32)
    coef = []
    for r in range(tiles):
        mass = jnp.where(owner == r, extra[r], mass)
    mass_ref[...] = mass
    for b in range(tiles // 8):
        coef.append(tile_of(extra[8 * b : 8 * b + 8]))
    coef.append(jnp.zeros((LANES - tiles, LANES), F32))
    coef = jnp.concatenate(coef, axis=0).T
    for r in range(tiles):
        at = 32 * ((r + 2) % 4)
        coef_ref[r, :, :] = jnp.broadcast_to(coef[at : at + 32, r : r + 1], (32, LANES))
    zero = jnp.zeros((8, LANES), F32)
    for b in range(4):
        place = slice(8 * b, 8 * b + 8)

        def step(_, field):
            out = []
            for r in range(tiles):
                up = field[r - 1] if r > 0 else zero
                down = field[r + 1] if r < tiles - 1 else zero
                out.append(field[r] + coef_ref[r, place, :] * (up + down - 2.0 * field[r]))
            return tuple(out)

        field = lax.fori_loop(
            0, HEAT_STEPS, step, tuple(msg_ref[PART * r + 8 * b : PART * r + 8 * b + 8, :] for r in range(tiles))
        )
        for r in range(tiles):
            field_ref[32 * r + 8 * b : 32 * r + 8 * b + 8, :] = field[r]
    smooth = lax.dot_general(
        patch_ref[...], field_ref[...], NT, preferred_element_type=F32, precision=EXACT
    )
    kernel = jnp.exp(EXPONENT_GAIN * smooth)
    kt_ref[...] = kernel
    short_ref[...] = jnp.minimum(kernel, BF16_MAX).astype(BF16)
    tile = row_partials(kt_ref, None)
    for g in range(out_ref.shape[0]):
        out_ref[g, 0:8, :] = tile
        out_ref[g, 8:16, :] = jnp.broadcast_to(weight_ref[...], (8, LANES))


def row_scale(msg_ref, mass_ref):
    total = msg_ref[0, 0:8, :]
    for g in range(1, msg_ref.shape[0]):
        total = total + msg_ref[g, 0:8, :]
    return mass_ref[...] / total


def scaled_columns(kt_ref, scale):
    pieces = [kt_ref[:, t * LANES : (t + 1) * LANES].astype(F32) for t in range(8)]
    return [piece * scale[t : t + 1, :] for t, piece in enumerate(pieces)]


def column_partials(kt_ref, scale):
    total = functools.reduce(lambda a, b: a + b, scaled_columns(kt_ref, scale))
    return jnp.sum(total.T, axis=0, keepdims=True)


def by_distance(msg_ref):
    groups = msg_ref.shape[0]
    me = lax.axis_index("grp")
    return tile_of([msg_ref[lax.rem(me + groups - k, groups), 8:9, :] for k in range(groups)])


def row_kernel(msg_ref, mass_ref, kt_ref, out_ref, weights_ref):
    weights_ref[...] = by_distance(msg_ref)
    column = column_partials(kt_ref, row_scale(msg_ref, mass_ref))
    for t in range(out_ref.shape[0]):
        out_ref[t, :, :] = column


def send_wide(out_ref, kernel_refs, scale):
    tile = tile_of([column_partials(ref, scale) for ref in kernel_refs])
    for t in range(out_ref.shape[0]):
        out_ref[t, :, :] = tile


def choose_kernel(even_ref, odd_ref, out_ref):
    odd = lax.rem(lax.axis_index("tile"), 2)

    @pl.when(odd == 0)
    def _():
        out_ref[...] = even_ref[...]

    @pl.when(odd == 1)
    def _():
        out_ref[...] = odd_ref[...]


def wide_row_sums(scale, kernel_refs):
    total = jnp.zeros((8, LANES), F32)
    for k, ref in enumerate(kernel_refs):
        total = total + row_partials(ref, column_of(scale[k : k + 1, :]))
    return total


def wide_row_kernel(msg_ref, mass_ref, *refs):
    kernel_refs, out_ref, later_ref = refs[:-2], refs[-2], refs[-1]
    scale = row_scale(msg_ref, mass_ref)
    send_wide(out_ref, kernel_refs, scale)
    later_ref[...] = scale * wide_row_sums(by_distance(msg_ref), kernel_refs)


def wide_row_scale(msg_ref, later_ref, weights_ref, kernel_refs):
    scale = column_scale([msg_ref[t] for t in range(msg_ref.shape[0])], weights_ref[...])
    return later_ref[...] / wide_row_sums(scale, kernel_refs)


def wide_round_kernel(msg_ref, later_ref, weights_ref, *refs):
    scale = wide_row_scale(msg_ref, later_ref, weights_ref, refs[:-1])
    send_wide(refs[-1], refs[:-1], scale)


def column_scale(parts, weight):
    while len(parts) > 1:
        parts = [a + b for a, b in zip(parts[0::2], parts[1::2])]
    return weight / parts[0]


def column_kernel(msg_ref, weight_ref, kt_ref, out_ref):
    scale = column_scale([msg_ref[t] for t in range(msg_ref.shape[0])], weight_ref[...])
    tile = row_partials(kt_ref, column_of(scale))
    for g in range(out_ref.shape[0]):
        out_ref[g, 0:8, :] = tile
        out_ref[g, 8:16, :] = jnp.broadcast_to(scale, (8, LANES))


def last_round_kernel(msg_ref, later_ref, weights_ref, *refs):
    out_ref = refs[-1]
    scale = wide_row_scale(msg_ref, later_ref, weights_ref, refs[:-1])
    pieces = scaled_columns(refs[0], scale)
    column = jnp.zeros((1, LANES), F32)
    for t in range(8):
        turned = pieces[t].T
        column = column + jnp.sum(turned, axis=0, keepdims=True)
        for r in range(4):
            at = PART * (4 * t + r)
            out_ref[at : at + 32, :] = turned[32 * r : 32 * r + 32]
    for at in range(32, out_ref.shape[0], PART):
        out_ref[at : at + 1, :] = column


def plan_kernel(cell_count, msg_ref, weight_ref, out_ref):
    tiles = msg_ref.shape[0] // PART
    sums = [msg_ref[PART * t + 32 : PART * t + 33, :] for t in range(tiles)]
    scale = column_scale(sums, weight_ref[...]) * cell_count
    for d in range(tiles):
        out_ref[0, 32 * d : 32 * d + 32, :] = msg_ref[PART * d : PART * d + 32, :] * scale


def swap(values, axis):
    return lax.all_to_all(values, axis, split_axis=0, concat_axis=0, tiled=True)


def swap_parts(parts, axis):
    size = lax.axis_size(axis)
    return swap(parts.reshape(size, PART, 1, LANES), axis).reshape(size * PART, LANES)


def body(spot_terms, spot_weight, spot_owner, spot_cell, col_coef, row_coef, tgt_coef, tgt_weight):
    tiles = lax.axis_size("tile")
    groups = lax.axis_size("grp")
    spots, columns = spot_terms.shape
    cells = col_coef.shape[1]
    shape = jax.ShapeDtypeStruct
    weight = tgt_weight.reshape(1, columns)

    packed = call(
        pack_kernel,
        shape((tiles, CAP + META, columns), BF16),
        [
            spot_owner.reshape(1, spots),
            spot_cell.reshape(1, spots),
            spot_weight.reshape(spots // LANES, LANES),
            spot_terms,
        ],
        scratch=[
            pltpu.VMEM((tiles, CAP + META, columns), BF16),
            pltpu.VMEM((256, spots), BF16),
            pltpu.VMEM((1, spots), jnp.int32),
            pltpu.VMEM((1, spots), jnp.int32),
            pltpu.VMEM((spots // LANES, LANES), BF16),
            pltpu.VMEM((spots, columns), BF16),
            pltpu.SemaphoreType.DMA((4,)),
            pltpu.SemaphoreType.DMA((tiles * CAP // 256,)),
        ],
        hbm=(0, 1, 2, 3),
        out_hbm=True,
    )
    ccol, patch = call(
        prep_kernel,
        (shape((cells, LANES), F32), shape((LANES, LANES), F32)),
        [col_coef, tgt_coef.reshape(1, columns)],
    )
    rcoef = jnp.tile(row_coef.reshape(tiles, 32), (1, LANES // 32))
    got = swap(packed, "tile")
    sorted_field = call(
        gather_kernel,
        shape((tiles * PART, LANES), F32),
        [got, ccol, rcoef],
        scratch=[
            pltpu.VMEM((256, tiles * CAP), BF16),
            pltpu.VMEM((cells + 16, LANES), F32),
            pltpu.VMEM((cells + 16, LANES), F32),
        ],
    )
    band = swap_parts(sorted_field, "tile")
    tile = shape((8, LANES), F32)
    wide = shape((tiles, groups, LANES), F32)
    field = (columns, cells)
    kt, short, mass, rows = call(
        band_kernel,
        (shape(field, F32), shape(field, BF16), tile, shape((groups, 16, LANES), F32)),
        [band, patch, weight],
        scratch=[pltpu.VMEM((tiles, 32, LANES), F32), pltpu.VMEM((cells, LANES), F32)],
    )
    up = [(g, (g + 1) % groups) for g in range(groups)]
    down = [(g, (g - 1) % groups) for g in range(groups)]
    before = [kt, lax.ppermute(short, "grp", up)]
    after = [kt, lax.ppermute(short, "grp", down)]


    def forward(value):
        value, last, first = lax.optimization_barrier((value, before[-1], after[-1]))
        before[-1], after[-1] = last, first
        before.append(lax.ppermute(last, "grp", up))
        after.append(lax.ppermute(first, "grp", down))
        return value

    rows = forward(swap(rows, "grp"))
    leap = [
        (g * tiles + t, (g - 3 + 6 * (t % 2)) % groups * tiles + t)
        for g in range(groups)
        for t in range(tiles)
    ]
    opposite = call(choose_kernel, shape(field, BF16), [after[1], before[1]])
    opposite = lax.ppermute(opposite, ("grp", "tile"), leap)
    cols, weights = call(row_kernel, (shape((tiles, 1, LANES), F32), tile), [rows, mass, kt])
    cols = forward(swap(cols, "tile"))
    rows = call(column_kernel, shape((groups, 16, LANES), F32), [cols, weight, kt])
    rows, opposite = lax.optimization_barrier((rows, opposite))
    rows = swap(rows, "grp")
    every = before + [opposite] + after[:0:-1]
    cols, later = call(wide_row_kernel, (wide, tile), [rows, mass] + every)
    for _ in range(SCALING_ROUNDS - 3):
        cols = swap(cols, "tile")
        cols = call(wide_round_kernel, wide, [cols, later, weights] + every)
    cols = swap(cols, "tile")
    scaled = call(
        last_round_kernel, shape((tiles * PART, LANES), F32), [cols, later, weights] + every
    )
    scaled = swap_parts(scaled, "tile")
    return call(
        functools.partial(plan_kernel, float(cells * tiles)),
        shape((1, cells, LANES), F32),
        [scaled, weight],
    )


def solution(mesh):
    return jax.shard_map(
        body,
        mesh=mesh,
        in_specs=(
            P("tile", "grp"),
            P("tile"),
            P("tile", None),
            P("tile"),
            P("tile", None),
            P("tile", None),
            P("grp"),
            P("grp"),
        ),
        out_specs=P("tile", None, "grp"),
        check_vma=False,
    )
```
